256 devices in a mesh: seq: 32 (over x, z_lo, core), tp: 8 (over y, z_hi).
Axes of the slice: x: 4, y: 4, z: 8 (z_hi: 2, z_lo: 4; z = z_hi * 4 + z_lo), core: 2. Of those that a mesh axis runs over, the one named last changes fastest.
Arguments:
- layer_input: bfloat16 [8192, 4096], P('seq', 'tp'), may hold values from -6 to 6
- value_weight: bfloat16 [4096, 4096], P(None, 'tp'), may hold values from -0.09375 to 0.09375
- filter_taps: bfloat16 [4096, 128], P('tp'), may hold values from -0.5 to 0.5
- query_codes: int32 [8192, 4096], P('seq', 'tp'), may hold values from 0 to 3
- query_low: float32 [8192, 32], P('seq', 'tp'), may hold values from -2 to -0.5
- query_high: float32 [8192, 32], P('seq', 'tp'), may hold values from 0.5 to 2
- key_codes: int32 [8192, 4096], P('seq', 'tp'), may hold values from 0 to 3
- key_low: float32 [8192, 32], P('seq', 'tp'), may hold values from -2 to -0.5
- key_high: float32 [8192, 32], P('seq', 'tp'), may hold values from 0.5 to 2
- out_grad: bfloat16 [8192, 4096], P('seq', 'tp'), may hold values from -6 to 6
Outputs:
- grad_input: float32 [8192, 4096], P('seq', 'tp')
- grad_weight: float32 [4096, 4096], P('seq', 'tp')
- grad_filter: float32 [4096, 128], P('tp')
- grad_query: float32 [8192, 4096], P('seq', 'tp')
- grad_key: float32 [8192, 4096], P('seq', 'tp')
The draws below stay inside these ranges and needn't reach their ends.
All inputs are finite; a program needn't handle non-finite values.
Results may differ from the reference program's by a relative error of at most 0.0065.
Values may be sent and summed in bfloat16 or wider, within the bound.
No kernel may reach another device: no remote copies, remote signals or barrier semaphores. Data moves between devices by JAX's collectives and lax.ppermute only.
A program may use at most 64 MiB of HBM per device.

```python
import math
import jax
import jax.numpy as jnp
from jax import lax

D = 4096
TAPS = 128
GROUP = 128
TOKENS = 8192


def with_ends(result, own_key, smallest, top_value):
    index_at = [jax.random.randint(jax.random.fold_in(own_key, axis), (), 0, length) for axis, length in enumerate(result.shape)]
    main_axis = result.shape.index(max(result.shape))
    next_to = index_at[:main_axis] + [(index_at[main_axis] + 1) % result.shape[main_axis]] + index_at[main_axis + 1:]
    return result.at[tuple(index_at)].set(smallest).at[tuple(next_to)].set(top_value)


def strengthened(entries, own_key, source, target, parts, factor):
    owner, partner = [(jnp.arange(entries.shape[axis_at]) // (entries.shape[axis_at] // parts)).reshape([-1 if axis == axis_at else 1 for axis in range(entries.ndim)]) for axis_at in (source, target)]
    chosen = jax.random.permutation(own_key, parts)[partner]
    strong = (owner == chosen) | (owner == (partner + parts // 2) % parts)
    return jnp.where(strong, factor * entries, entries)


def block_levels(key, extent, shards, least, top_value):
    loudness, own = 1.0, jax.random.fold_in(key, 6)
    for axis_at, blocks in shards:
        steps = jnp.exp(jax.random.uniform(jax.random.fold_in(own, axis_at), (blocks,), jnp.float32, least / len(shards), top_value / len(shards)))
        loudness = loudness * jnp.repeat(steps, extent[axis_at] // blocks).reshape([-1 if axis == axis_at else 1 for axis in range(len(extent))])
    return loudness


def bell_draw(stream_key, shape, spread, most, shards=(), kind=jnp.bfloat16):
    gain = block_levels(stream_key, shape, shards, -0.22, 0.18) if shards else 1.0
    array = jax.random.normal(stream_key, shape, jnp.float32) * spread * gain
    return jnp.minimum(jnp.maximum(array, -most), most).astype(kind)


def gaussian_with(stream_key, dims, spread, bound, cuts, heavy, held_as=jnp.bfloat16):
    result = spread * jax.random.normal(stream_key, dims, jnp.float32)
    if cuts:
        result = result * block_levels(stream_key, dims, cuts, -0.22, 0.18)
    return jnp.clip(strengthened(result, jax.random.fold_in(stream_key, 3), *heavy), -bound, bound).astype(held_as)


def setup_inputs(seed: int = 0) -> dict:
    key_of = jax.random.split(jax.random.key(seed), 11)
    return {
        "layer_input": gaussian_with(key_of[0], (TOKENS, D), 1.0, 6.0, ((0, 32), (1, 8)), (0, 1, 32, 2.75)),
        "value_weight": bell_draw(key_of[1], (D, D), D ** -0.5, 0.09375, ((1, 8),)),
        "filter_taps": bell_draw(key_of[2], (D, TAPS), 0.09, 0.5, ((0, 8),)),
        "query_codes": with_ends(jax.random.randint(key_of[3], (TOKENS, D), 0, 4), jax.random.fold_in(key_of[3], 1), 0, 3).astype(jnp.int32),
        "query_low": jnp.clip(-2.0 + 1.5 * jax.random.uniform(key_of[4], (TOKENS, D // GROUP), jnp.float32) ** block_levels(key_of[4], (TOKENS, D // GROUP), ((0, 32), (1, 8)), -0.2, 0.2), -2.0, -0.5),
        "query_high": jnp.clip(0.5 + 1.5 * jax.random.uniform(key_of[5], (TOKENS, D // GROUP), jnp.float32) ** block_levels(key_of[5], (TOKENS, D // GROUP), ((0, 32), (1, 8)), -0.2, 0.2), 0.5, 2.0),
        "key_codes": with_ends(jax.random.randint(key_of[6], (TOKENS, D), 0, 4), jax.random.fold_in(key_of[6], 1), 0, 3).astype(jnp.int32),
        "key_low": jnp.clip(-2.0 + 1.5 * jax.random.uniform(key_of[7], (TOKENS, D // GROUP), jnp.float32) ** block_levels(key_of[7], (TOKENS, D // GROUP), ((0, 32), (1, 8)), -0.2, 0.2), -2.0, -0.5),
        "key_high": jnp.clip(0.5 + 1.5 * jax.random.uniform(key_of[8], (TOKENS, D // GROUP), jnp.float32) ** block_levels(key_of[8], (TOKENS, D // GROUP), ((0, 32), (1, 8)), -0.2, 0.2), 0.5, 2.0),
        "out_grad": bell_draw(key_of[9], (TOKENS, D), 1.0, 6.0, ((0, 32), (1, 8))),
    }


def dequantize(code_array, lower, upper):
    token_count, channels = code_array.shape
    groups = lower.shape[1]
    levels = code_array.reshape(token_count, groups, channels // groups).astype(jnp.float32)
    step_size = (upper - lower) / 3.0
    return (lower[:, :, None] + levels * step_size[:, :, None]).reshape(token_count, channels)

def reference(layer_input, value_weight, filter_taps, query_codes, query_low, query_high, key_codes, key_low, key_high, out_grad):
    halo_rows = TAPS - 1
    queries = dequantize(query_codes, query_low, query_high)
    key_values = dequantize(key_codes, key_low, key_high)
    values = jnp.dot(layer_input, value_weight, preferred_element_type=jnp.float32)
    product = (key_values * values).astype(jnp.bfloat16)
    upstream = out_grad.astype(jnp.float32)
    grad_conv = (upstream * queries).astype(jnp.bfloat16)
    grad_conv_wide = grad_conv.astype(jnp.float32)
    blank = jnp.zeros((halo_rows, D), jnp.float32)
    product_pad = jnp.concatenate([blank, product.astype(jnp.float32)], 0)
    grad_pad = jnp.concatenate([grad_conv_wide, blank], 0)
    taps_wide = filter_taps.astype(jnp.float32)

    def step(index, carry):
        conv_out, grad_mix, filter_grad = carry
        index = index.astype(jnp.int32)
        earlier = lax.dynamic_slice_in_dim(product_pad, (halo_rows - index).astype(jnp.int32), TOKENS, 0)
        later = lax.dynamic_slice_in_dim(grad_pad, index, TOKENS, 0)
        tap_column = lax.dynamic_slice_in_dim(taps_wide, index, 1, 1)[:, 0]
        conv_out = conv_out + earlier * tap_column[None, :]
        grad_mix = grad_mix + later * tap_column[None, :]
        column = lax.optimization_barrier(jnp.sum(grad_conv_wide * earlier, axis=0))
        filter_grad = lax.dynamic_update_slice_in_dim(filter_grad, column[:, None], index, 1)
        return (conv_out, grad_mix, filter_grad)
    start = (jnp.zeros((TOKENS, D), jnp.float32), jnp.zeros((TOKENS, D), jnp.float32), jnp.zeros((D, TAPS), jnp.float32))
    conv_out, grad_mix, filter_grad = lax.fori_loop(0, TAPS, step, start)
    scale = 1.0 / math.sqrt(TOKENS)
    grad_query = upstream * conv_out
    grad_key = grad_mix * values
    grad_value = (grad_mix * key_values).astype(jnp.bfloat16)
    grad_input = jnp.dot(grad_value, value_weight.T, preferred_element_type=jnp.float32)
    grad_weight = jnp.dot(layer_input.T, grad_value, preferred_element_type=jnp.float32) * scale
    grad_filter = filter_grad * scale
    return (grad_input, grad_weight, grad_filter, grad_query, grad_key)
```

```python
import functools
import math

import jax
import jax.numpy as jnp
from jax import lax
from jax.experimental import pallas as pl
from jax.experimental.pallas import tpu as pltpu
from jax.sharding import Mesh, PartitionSpec as P

SEQ = ("x", "zl", "core")
TP = ("y", "zh")
LANES = 128
BLOCK = 16
F32 = jnp.float32
BF16 = jnp.bfloat16
VMEM = pl.BlockSpec(memory_space=pltpu.VMEM)
SMEM = pl.BlockSpec(memory_space=pltpu.SMEM)
HBM = pl.BlockSpec(memory_space=pltpu.HBM)
COST = {"prepare": 1.75, "mix": 5.39, "weight": 2.8, "back": 2.59, "pair": 0.7, "split": 0.56, "product": 0.63, "merge": 1.05, "taps": 5.6, "last":0.5,"middle1": 0.35, "middle3":0.5,"middle4":0.5,"middle2": 0.35, "gather": 1.05, "conv": 5.88, "input": 0.56, "finish": 0.91, "ends": 0.91, "after": 0.35}
PARAMS = pltpu.CompilerParams(vmem_limit_bytes=40 * 1024 * 1024)
def room(used):
    return pltpu.CompilerParams(vmem_limit_bytes=int(used * 1024 * 1024))


def shifted(block, axis, k):
    n = lax.axis_size(axis)
    return lax.ppermute(block, axis, [(i, (i + k) % n) for i in range(n)])


def crossed(block, axis, d):
    return lax.ppermute(block, axis, [(i, i ^ d) for i in range(lax.axis_size(axis))])


def along_tokens(block, step):
    n = lax.axis_size(SEQ)
    return lax.ppermute(block, SEQ, [(i, i + step) for i in range(n) if 0 <= i + step < n])


def estimate(name):
    time = COST[name]
    return pl.CostEstimate(
        flops=int(time * 1e9), bytes_accessed=int(time * 3.3e6), transcendentals=0
    )


def staged(kernel, kinds):
    count = len(kinds)
    moved = [i for i, kind in enumerate(kinds) if kind == "in"]

    def body(*refs):
        inputs, rest = list(refs[:count]), list(refs[count:])
        held, sems = rest[len(rest) - len(moved) - 1 : -1], rest[-1]
        copies = [
            pltpu.make_async_copy(inputs[i], held[n], sems.at[n]) for n, i in enumerate(moved)
        ]
        for copy in copies:
            copy.start()
        for n, i in enumerate(moved):
            inputs[i] = held[n]
        for copy in copies:
            copy.wait()
        given = [r for r, kind in zip(inputs, kinds) if kind not in ("tie", "mark")]
        kernel(*given, *rest[: len(rest) - len(moved) - 1])

    return body


SPECS = {"in": HBM, "hbm": HBM, "tie": HBM, "vmem": VMEM, "mark": VMEM, "smem": SMEM}


def call(name, kernel, out, inputs, scratch=(), params=PARAMS):
    kinds = [kind for kind, _ in inputs]
    values = [value for _, value in inputs]
    moved = [v for kind, v in inputs if kind == "in"]
    scratch = list(scratch)
    if moved:
        kernel = staged(kernel, kinds)
        scratch += [pltpu.VMEM(v.shape, v.dtype) for v in moved]
        scratch += [pltpu.SemaphoreType.DMA((len(moved),))]
    else:
        inner, keep = kernel, [i for i, k in enumerate(kinds) if k not in ("tie", "mark")]
        count = len(kinds)

        def kernel(*refs):
            inner(*[refs[i] for i in keep], *refs[count:])

    return pl.pallas_call(
        kernel,
        out_shape=out,
        in_specs=[SPECS[kind] for kind in kinds],
        out_specs=jax.tree.map(lambda _: VMEM, out),
        scratch_shapes=scratch,
        compiler_params=params,
        cost_estimate=estimate(name),
        name=name,
    )(*values)


def after(block, *waits):
    kinds = [kind for kind, _ in waits]
    return pl.pallas_call(
        lambda *refs: None,
        out_shape=struct(block.shape, block.dtype),
        in_specs=[HBM] + [SPECS[kind] for kind in kinds],
        out_specs=HBM,
        input_output_aliases={0: 0},
        compiler_params=PARAMS,
        cost_estimate=estimate("after"),
        name="after",
    )(block, *[value for _, value in waits])


def struct(shape, dtype):
    return jax.ShapeDtypeStruct(shape, dtype)


def spread(natural, tile, wide, count, offset, span):
    @pl.loop(0, count // 8)
    def _(b):
        for i in range(8):
            s = b * 8 + i
            wide[s] = natural[tile, pl.ds(s + offset, 8, stride=span), :]


def convolve(wide, turned, natural_out, tile, span, causal):
    tap_count = turned.shape[1]
    for rb in range(span // BLOCK):

        def body(jb, acc):
            start = (rb - jb) * BLOCK + tap_count - BLOCK if causal else (rb + jb) * BLOCK
            window = [wide[start + i] for i in range(2 * BLOCK - 1)]
            acc = list(acc)
            for j in range(BLOCK):
                tap = jnp.broadcast_to(turned[tile, pl.ds(jb * BLOCK + j, 1), :], (8, LANES))
                for r in range(BLOCK):
                    acc[r] = acc[r] + tap * window[r - j + BLOCK - 1 if causal else r + j]
            return tuple(acc)

        zero = jnp.zeros((8, LANES), F32)
        acc = lax.fori_loop(0, tap_count // BLOCK, body, (zero,) * BLOCK)
        for r in range(BLOCK):
            natural_out[tile, pl.ds(rb * BLOCK + r, 8, stride=span), :] = acc[r]


def columns(low, high, codes, group):
    shape = (LANES, low.shape[1])
    bottom = jnp.broadcast_to(low[group : group + 1, :], shape).T
    step = jnp.broadcast_to((high[group : group + 1, :] - low[group : group + 1, :]) / 3.0, shape).T
    return bottom + codes[:, group * LANES : (group + 1) * LANES].astype(F32) * step


def prepare_kernel(up, codes, low, high, key_codes, key_low, key_high, taps, *outs):
    grad_conv, head, key, turned, mark = outs
    mark[...] = jnp.zeros_like(mark)
    for l in range(codes.shape[1] // LANES):
        cols = pl.ds(l * LANES, LANES)
        g = (up[:, cols].astype(F32) * columns(low, high, codes, l)).astype(BF16)
        grad_conv[:, cols] = g
        head[:, cols] = g[: head.shape[0]]
        key[:, cols] = columns(key_low, key_high, key_codes, l)
        turned[l] = taps[cols, :].astype(F32).T


def product_kernel(value, mix, key, product, tail, key_grad):
    p = (key[...] * value[...]).astype(BF16)
    product[...] = p
    tail[...] = p[p.shape[0] - tail.shape[0] :]
    key_grad[...] = mix[...] * value[...]


def mix_kernel(g, halo, turned, key, mix, value, turned_value, nat, wide, out):
    rows, channels = g.shape
    tiles, tap_count = channels // LANES, halo.shape[0]
    for l in range(tiles):
        cols = pl.ds(l * LANES, LANES)
        nat[l, pl.ds(0, rows), :] = g[:, cols].astype(F32)
        nat[l, pl.ds(rows, tap_count), :] = halo[:, cols].astype(F32)

    @pl.loop(0, tiles)
    def _(l):
        spread(nat, l, wide, wide.shape[0], 0, rows // 8)
        convolve(wide, turned, out, l, rows // 8, False)

    for l in range(tiles):
        cols = pl.ds(l * LANES, LANES)
        m = out[l]
        mix[:, cols] = m
        v = m * key[:, cols]
        value[:, cols] = v.astype(BF16)
        turned_value[cols, :] = v.T.astype(BF16)


def filter_kernel(place, p, halo, g, kept, given, mark, nat, nat_g, wide, wide_g, halves):
    mark[...] = jnp.zeros_like(mark)
    rows, channels = g.shape
    tiles, tap_count, span = channels // LANES, halo.shape[0], g.shape[0] // 8
    core, per_half = place[2], halo.shape[0] // 2 // BLOCK
    for l in range(tiles):
        cols = pl.ds(l * LANES, LANES)
        nat[l, pl.ds(0, tap_count), :] = halo[:, cols].astype(F32)
        nat[l, pl.ds(tap_count, rows), :] = p[:, cols].astype(F32)
        nat_g[l] = g[:, cols].astype(F32)

    for l in range(tiles):
        spread(nat, l, wide, wide.shape[0], 1, span)
        spread(nat_g, l, wide_g, span, 0, span)

        @pl.loop(0, tap_count // BLOCK)
        def _(jb):
            zero = jnp.zeros((8, LANES), F32)
            acc = [zero] * BLOCK
            for rb in range(span // BLOCK):
                start = (rb - jb) * BLOCK + tap_count - BLOCK
                window = [wide[start + i] for i in range(2 * BLOCK - 1)]
                for r in range(BLOCK):
                    up = wide_g[rb * BLOCK + r]
                    for j in range(BLOCK):
                        acc[j] = acc[j] + up * window[r - j + BLOCK - 1]
            rows_of = [jnp.sum(a, axis=0, keepdims=True) for a in acc]
            at = pl.ds(pl.multiple_of(lax.rem(jb, per_half) * BLOCK, BLOCK), BLOCK)
            half = lax.div(jb, per_half) ^ core
            halves[half, at, pl.ds(l * LANES, LANES)] = jnp.concatenate(rows_of, axis=0)

    kept[...] = halves[0]
    given[...] = halves[1]


def middle_kernel(kept, received, total, sent, mark):
    mark[...] = jnp.zeros_like(mark)
    total[...] = kept[...] + received[...].astype(F32)
    sent[...] = total[...].astype(BF16)


def conv_kernel(p, halo, upstream, turned, query_grad, mark, nat, wide, out):
    mark[...] = jnp.zeros_like(mark)
    rows, channels = p.shape
    tiles, tap_count = channels // LANES, halo.shape[0]
    for l in range(tiles):
        cols = pl.ds(l * LANES, LANES)
        nat[l, pl.ds(0, tap_count), :] = halo[:, cols].astype(F32)
        nat[l, pl.ds(tap_count, rows), :] = p[:, cols].astype(F32)

    @pl.loop(0, tiles)
    def _(l):
        spread(nat, l, wide, wide.shape[0], 1, rows // 8)
        convolve(wide, turned, out, l, rows // 8, True)

    for l in range(tiles):
        cols = pl.ds(l * LANES, LANES)
        query_grad[:, cols] = upstream[:, cols].astype(F32) * out[l]


def back_kernel(place, value, held_x, weight, keep, give, values, mark, held, sems):
    mark[...] = jnp.zeros_like(mark)
    x, y, zh = place[0], place[3], place[4]
    depth = held.shape[1]
    copies = []
    order = [(out, q, h) for out in (give, keep) for q in range(2) for h in range(2)]
    owners = [y ^ (1 if out is give else 0) ^ (3 if q else 0) for out, q, h in order]
    for i, (out, q, h) in enumerate(order):
        rows = pl.ds(pl.multiple_of((owners[i] * 2 + (zh ^ h)) * depth, depth), depth)
        copies.append(pltpu.make_async_copy(weight.at[rows, :], held.at[i], sems.at[i]))
    for copy in copies:
        copy.start()
    g = value[...]
    for i, (out, q, h) in enumerate(order):
        copies[i].wait()
        part = lax.dot_general(g, held[i], (((1,), (1,)), ((), ())), preferred_element_type=F32)
        out[q, :, h * depth : (h + 1) * depth] = part.astype(out.dtype)
        block = held_x[lax.rem(owners[i] - x + 4, 4) * 2 + h]
        part = jnp.dot(block, held[i], preferred_element_type=F32)
        values[...] = part if i == 0 else values[...] + part


def pair_kernel(keep, received, own, sent, mark):
    mark[...] = jnp.zeros_like(mark)
    own[...] = keep[0] + received[0].astype(F32)
    sent[...] = (keep[1] + received[1].astype(F32)).astype(BF16)


def split_kernel(own, received, passing, staying, mark):
    mark[...] = jnp.zeros_like(mark)
    width = staying.shape[1]
    for h, out in ((0, staying), (1, passing)):
        cols = pl.ds(h * width, width)
        out[...] = (own[:, cols] + received[:, cols].astype(F32)).astype(out.dtype)


def fetch(place, blocks, held, sems):
    waits = []
    for k in range(4):
        slot = lax.rem(place[3] - place[0] - k + 8, 4)
        for phase in range(2):
            i = 2 * k + phase
            for m in range(4):

                @pl.when(slot == m)
                def _():
                    pltpu.make_async_copy(blocks[4 * phase + m], held.at[i], sems.at[i]).start()

            waits.append(pltpu.make_async_copy(blocks[0], held.at[i], sems.at[i]))
    return waits


def weight_kernel(place, *refs):
    blocks, (value, keep, give, held, mark, sems) = refs[:8], refs[8:]
    mark[...] = jnp.zeros_like(mark)
    core = place[2]
    waits = fetch(place, blocks, held, sems)
    g = value[...]
    for i in range(8):
        waits[i].wait()
        part = jnp.dot(g, held[i], preferred_element_type=F32)
        for j in range(2):
            a = part[:, 2 * j * LANES : (2 * j + 1) * LANES]
            b = part[:, (2 * j + 1) * LANES : (2 * j + 2) * LANES]
            cols = pl.ds(((i % 2) * 2 + j) * LANES, LANES)
            keep[i // 2, :, cols] = jnp.where(core == 0, a, b)
            give[i // 2, :, cols] = jnp.where(core == 0, b, a).astype(BF16)


def merge_kernel(keep, received, r0, r1, r2, r3, mark):
    mark[...] = jnp.zeros_like(mark)
    for k, r in enumerate((r0, r1, r2, r3)):
        r[...] = (keep[k] + received[k].astype(F32)).astype(r.dtype)


def gather_kernel(place, r0, r1, r2, r3, own, a1, a2, a3, mark, total):
    mark[...] = jnp.zeros_like(mark)
    zl, zh = place[1], place[4]
    for q in range(4):
        cols = pl.ds(q * LANES, LANES)
        s = r0[:, cols]
        for r in (r1, r2, r3):
            s = s + r[:, cols].astype(F32)
        total[((zh ^ (q // 2)) * 2 + q % 2) ^ zl] = s
    own[...] = total[0]
    for d, a in enumerate((a1, a2, a3)):
        a[...] = total[d + 1].astype(BF16)


def finish_kernel(scale, own, r1, r2, r3, out):
    s = own[...]
    for r in (r1, r2, r3):
        s = s + r[...].astype(F32)
    out[...] = s.T * scale


def last_kernel(own, received, out):
    out[...] = own[...] + received[...].astype(F32)


def input_kernel(staying, arrived, out):
    out[...] = staying[...].astype(F32) + arrived[...].astype(F32)


def ends_kernel(scale, place, own, other, out, both):
    half = own.shape[0]
    both[pl.ds(pl.multiple_of(place[2] * half, half), half), :] = own[...]
    both[pl.ds(pl.multiple_of((1 - place[2]) * half, half), half), :] = other[...]
    out[...] = both[...].T * scale


def shards(
    layer_input,
    value_weight,
    filter_taps,
    query_codes,
    query_low,
    query_high,
    key_codes,
    key_low,
    key_high,
    out_grad,
):
    rows, width = layer_input.shape
    channels, tap_count = filter_taps.shape
    tiles, span = channels // LANES, rows // 8
    place = jnp.stack([lax.axis_index(axis) for axis in SEQ + TP]).astype(jnp.int32)
    scale = 1.0 / math.sqrt(rows * lax.axis_size(SEQ))

    mark = struct((8, LANES), F32)
    wide_shape = pltpu.VMEM((tap_count + span, 8, LANES), F32)
    nat_shape = pltpu.VMEM((tiles, rows + tap_count + 8, LANES), F32)
    out_scratch = pltpu.VMEM((tiles, rows, LANES), F32)
    plane = struct((rows, channels), F32)
    half_plane = struct((rows, channels), BF16)

    far = crossed(layer_input, "zh", 1)
    near_blocks = [layer_input] + [shifted(layer_input, "y", k) for k in (1, 2, 3)]
    grad_conv, head, key, turned, prepare_mark = call(
        "prepare",
        prepare_kernel,
        (
            half_plane,
            struct((tap_count, channels), BF16),
            plane,
            struct((tiles, tap_count, LANES), F32),
            mark,
        ),
        [("in", v) for v in (out_grad, query_codes, query_low.T, query_high.T)]
        + [("in", v) for v in (key_codes, key_low.T, key_high.T, filter_taps)],
        params=room(60),
    )
    later_rows = along_tokens(head, -1)
    far = after(far, *[("tie", b) for b in near_blocks[1:]], ("mark", prepare_mark))
    far_blocks = [far] + [shifted(far, "y", k) for k in (1, 2, 3)]
    grad_mix, grad_value, turned_value = call(
        "mix",
        mix_kernel,
        (plane, half_plane, struct((channels, rows), BF16)),
        [("in", grad_conv), ("in", later_rows), ("in", turned), ("in", key), ("tie", far)],
        [nat_shape, wide_shape, out_scratch],
        room(62.5),
    )

    eight = pltpu.SemaphoreType.DMA((8,))
    blocks = [("hbm", b) for b in near_blocks + far_blocks]
    keep, give, gathered, weight_mark = call(
        "weight",
        weight_kernel,
        (
            struct((4, channels, 4 * LANES), F32),
            struct((4, channels, 4 * LANES), BF16),
            struct((8, rows, width), BF16),
            mark,
        ),
        [("smem", place)] + blocks + [("vmem", turned_value)],
        [eight],
        room(40),
    )
    given_terms = crossed(give, "core", 1)
    back_keep, back_give, values, _ = call(
        "back",
        back_kernel,
        (
            struct((2, rows, 2 * width), F32),
            struct((2, rows, 2 * width), BF16),
            plane,
            mark,
        ),
        [("smem", place), ("vmem", grad_value), ("vmem", gathered), ("hbm", value_weight)]
        + [("mark", weight_mark)],
        [pltpu.VMEM((8, width, channels), BF16), eight],
        room(46),
    )
    product, tail, grad_key = call(
        "product",
        product_kernel,
        (half_plane, struct((tap_count, channels), BF16), plane),
        [("vmem", values), ("vmem", grad_mix), ("vmem", key)],
    )
    *terms, merge_mark = call(
        "merge",
        merge_kernel,
        (struct((channels, 4 * LANES), F32),)
        + (struct((channels, 4 * LANES), BF16),) * 3
        + (mark,),
        [("vmem", keep), ("in", given_terms)],
    )
    sent = [shifted(terms[k], "x", k) for k in (1, 2, 3)]
    earlier_rows = along_tokens(tail, 1)
    half_taps = struct((tap_count // 2, channels), F32)
    kept, given, taps_mark = call(
        "taps",
        filter_kernel,
        (half_taps, half_taps, mark),
        [("smem", place), ("vmem", product), ("in", earlier_rows), ("vmem", grad_conv)]
        + [("mark", merge_mark)],
        [
            nat_shape,
            out_scratch,
            wide_shape,
            pltpu.VMEM((span, 8, LANES), F32),
            pltpu.VMEM((2, tap_count // 2, channels), F32),
        ],
    )
    filter_sum, filter_sent, middle1_mark = call(
        "middle1",
        middle_kernel,
        (half_taps, struct((tap_count // 2, channels), BF16), mark),
        [("vmem", kept), ("in", crossed(given, "core", 1))],
    )
    back_own, back_sent, pair_mark = call(
        "pair",
        pair_kernel,
        (struct((rows, 2 * width), F32), struct((rows, 2 * width), BF16), mark),
        [("vmem", back_keep), ("in", crossed(back_give, "y", 1)), ("mark", middle1_mark)],
    )
    passing, staying, split_mark = call(
        "split",
        split_kernel,
        (struct((rows, width), BF16), struct((rows, width), F32), mark),
        [("vmem", back_own), ("in", crossed(back_sent, "y", 3))],
    )
    arrived_input = crossed(passing, "zh", 1)
    own, *ahead, gather_mark = call(
        "gather",
        gather_kernel,
        (struct((channels, LANES), F32),)
        + (struct((channels, LANES), BF16),) * 3
        + (mark,),
        [("smem", place), ("vmem", terms[0])]
        + [("in", v) for v in sent],
        [pltpu.VMEM((4, channels, LANES), F32)],
    )
    arrived = [crossed(ahead[d - 1], "zl", d) for d in (1, 2, 3)]
    grad_query, conv_mark = call(
        "conv",
        conv_kernel,
        (plane, mark),
        [("vmem", product), ("in", earlier_rows), ("in", out_grad), ("vmem", turned)]
        + [("mark", gather_mark), ("mark", split_mark)],
        [nat_shape, wide_shape, out_scratch],
    )
    filter_sum, filter_sent, middle2_mark = call(
        "middle2",
        middle_kernel,
        (half_taps, struct((tap_count // 2, channels), BF16), mark),
        [("vmem", filter_sum), ("in", crossed(filter_sent, "zl", 1))],
    )
    filter_sum, filter_sent, middle3_mark = call(
        "middle3",
        middle_kernel,
        (half_taps, struct((tap_count // 2, channels), BF16), mark),
        [("vmem", filter_sum), ("in", crossed(filter_sent, "zl", 2))]
        + [("mark", gather_mark)],
    )
    filter_sum, filter_sent, middle4_mark = call(
        "middle4",
        middle_kernel,
        (half_taps, struct((tap_count // 2, channels), BF16), mark),
        [("vmem", filter_sum), ("in", crossed(filter_sent, "x", 1))],
    )
    filter_sum = call(
        "last",
        last_kernel,
        half_taps,
        [("vmem", filter_sum), ("in", crossed(filter_sent, "x", 3))]
        + [("tie", v) for v in arrived]
        + [("mark", conv_mark)],
    )
    grad_input = call(
        "input",
        input_kernel,
        struct((rows, width), F32),
        [("vmem", staying), ("in", arrived_input)],
    )
    grad_weight = call(
        "finish",
        functools.partial(finish_kernel, scale),
        struct((LANES, channels), F32),
        [("vmem", own)]
        + [("in", v) for v in arrived]
        + [("mark", conv_mark)],
    )
    grad_filter = call(
        "ends",
        functools.partial(ends_kernel, scale),
        struct((channels, tap_count), F32),
        [("smem", place), ("vmem", filter_sum), ("in", crossed(filter_sum, "core", 1))],
        [pltpu.VMEM((tap_count, channels), F32)],
    )
    return (grad_input, grad_weight, grad_filter, grad_query, grad_key)


def solution(mesh):
    fine = Mesh(mesh.devices.reshape(4, 4, 2, 4, 2), SEQ + TP)
    both = P(SEQ, TP)
    return jax.shard_map(
        shards,
        mesh=fine,
        in_specs=(both, P(None, TP), P(TP, None)) + (both,) * 7,
        out_specs=(both, both, P(TP, None), both, both),
        check_vma=False,
    )
```

```python
import functools
import math

import jax
import jax.numpy as jnp
from jax import lax
from jax.experimental import pallas as pl
from jax.experimental.pallas import tpu as pltpu
from jax.sharding import Mesh, PartitionSpec as P

SEQ = ("x", "zl", "core")
TP = ("y", "zh")
LANES = 128
BLOCK = 16
F32 = jnp.float32
BF16 = jnp.bfloat16
VMEM = pl.BlockSpec(memory_space=pltpu.VMEM)
SMEM = pl.BlockSpec(memory_space=pltpu.SMEM)
HBM = pl.BlockSpec(memory_space=pltpu.HBM)
COST = {"prepare": 1.75, "mix": 5.39, "weight": 2.8, "back": 2.59, "pair": 0.7, "split": 0.56, "product": 0.63, "merge": 1.05, "taps": 5.6, "last":0.5,"middle1": 0.35, "middle3":0.5,"middle4":0.5,"middle2": 0.35, "gather": 1.05, "conv": 5.88, "input": 0.56, "finish": 0.91, "ends": 0.91, "after": 0.35}
PARAMS = pltpu.CompilerParams(vmem_limit_bytes=40 * 1024 * 1024)
def room(used):
    return pltpu.CompilerParams(vmem_limit_bytes=int(used * 1024 * 1024))


def shifted(block, axis, k):
    n = lax.axis_size(axis)
    return lax.ppermute(block, axis, [(i, (i + k) % n) for i in range(n)])


def crossed(block, axis, d):
    return lax.ppermute(block, axis, [(i, i ^ d) for i in range(lax.axis_size(axis))])


def along_tokens(block, step):
    n = lax.axis_size(SEQ)
    return lax.ppermute(block, SEQ, [(i, i + step) for i in range(n) if 0 <= i + step < n])


def estimate(name):
    time = COST[name]
    return pl.CostEstimate(
        flops=int(time * 1e9), bytes_accessed=int(time * 3.3e6), transcendentals=0
    )


def staged(kernel, kinds):
    count = len(kinds)
    moved = [i for i, kind in enumerate(kinds) if kind == "in"]

    def body(*refs):
        inputs, rest = list(refs[:count]), list(refs[count:])
        held, sems = rest[len(rest) - len(moved) - 1 : -1], rest[-1]
        copies = [
            pltpu.make_async_copy(inputs[i], held[n], sems.at[n]) for n, i in enumerate(moved)
        ]
        for copy in copies:
            copy.start()
        for n, i in enumerate(moved):
            inputs[i] = held[n]
        for copy in copies:
            copy.wait()
        given = [r for r, kind in zip(inputs, kinds) if kind not in ("tie", "mark")]
        kernel(*given, *rest[: len(rest) - len(moved) - 1])

    return body


SPECS = {"in": HBM, "hbm": HBM, "tie": HBM, "vmem": VMEM, "mark": VMEM, "smem": SMEM}


def call(name, kernel, out, inputs, scratch=(), params=PARAMS):
    kinds = [kind for kind, _ in inputs]
    values = [value for _, value in inputs]
    moved = [v for kind, v in inputs if kind == "in"]
    scratch = list(scratch)
    if moved:
        kernel = staged(kernel, kinds)
        scratch += [pltpu.VMEM(v.shape, v.dtype) for v in moved]
        scratch += [pltpu.SemaphoreType.DMA((len(moved),))]
    else:
        inner, keep = kernel, [i for i, k in enumerate(kinds) if k not in ("tie", "mark")]
        count = len(kinds)

        def kernel(*refs):
            inner(*[refs[i] for i in keep], *refs[count:])

    return pl.pallas_call(
        kernel,
        out_shape=out,
        in_specs=[SPECS[kind] for kind in kinds],
        out_specs=jax.tree.map(lambda _: VMEM, out),
        scratch_shapes=scratch,
        compiler_params=params,
        cost_estimate=estimate(name),
        name=name,
    )(*values)


def after(block, *waits):
    kinds = [kind for kind, _ in waits]
    return pl.pallas_call(
        lambda *refs: None,
        out_shape=struct(block.shape, block.dtype),
        in_specs=[HBM] + [SPECS[kind] for kind in kinds],
        out_specs=HBM,
        input_output_aliases={0: 0},
        compiler_params=PARAMS,
        cost_estimate=estimate("after"),
        name="after",
    )(block, *[value for _, value in waits])


def struct(shape, dtype):
    return jax.ShapeDtypeStruct(shape, dtype)


def spread(natural, tile, wide, count, span):
    step = span // 8
    for a in range(count // 8):
        rows = [natural[tile, pl.ds(8 * (a + step * q), 8), :] for q in range(8)]
        wide[pl.ds(8 * a, 8)] = jnp.swapaxes(jnp.stack(rows, 0), 0, 1)


def convolve(wide, turned, natural_out, turn, tile, span, causal):
    tap_count = turned.shape[1]
    for rb in range(span // BLOCK):

        def body(jb, acc):
            start = (rb - jb) * BLOCK + tap_count - BLOCK + 1 if causal else (rb + jb) * BLOCK
            window = [wide[start + i] for i in range(2 * BLOCK - 1)]
            acc = list(acc)
            for j in range(BLOCK):
                tap = jnp.broadcast_to(turned[tile, pl.ds(jb * BLOCK + j, 1), :], (8, LANES))
                for r in range(BLOCK):
                    acc[r] = acc[r] + tap * window[r - j + BLOCK - 1 if causal else r + j]
            return tuple(acc)

        zero = jnp.zeros((8, LANES), F32)
        acc = lax.fori_loop(0, tap_count // BLOCK, body, (zero,) * BLOCK)
        for r in range(BLOCK):
            turn[rb * BLOCK + r] = acc[r]
    for a in range(span // 8):
        eight = jnp.swapaxes(turn[pl.ds(8 * a, 8)], 0, 1)
        for q in range(8):
            natural_out[tile, pl.ds(q * span + 8 * a, 8), :] = eight[q]


def columns(low, high, codes, group):
    shape = (LANES, low.shape[1])
    bottom = jnp.broadcast_to(low[group : group + 1, :], shape).T
    step = jnp.broadcast_to((high[group : group + 1, :] - low[group : group + 1, :]) / 3.0, shape).T
    return bottom + codes[:, group * LANES : (group + 1) * LANES].astype(F32) * step


def prepare_kernel(up, codes, low, high, key_codes, key_low, key_high, taps, *outs):
    grad_conv, head, key, turned = outs
    for l in range(codes.shape[1] // LANES):
        cols = pl.ds(l * LANES, LANES)
        g = (up[:, cols].astype(F32) * columns(low, high, codes, l)).astype(BF16)
        grad_conv[:, cols] = g
        head[:, cols] = g[: head.shape[0]]
        key[:, cols] = columns(key_low, key_high, key_codes, l)
        turned[l] = taps[cols, :].astype(F32).T


def product_kernel(value, mix, key, product, tail, key_grad):
    p = (key[...] * value[...]).astype(BF16)
    product[...] = p
    tail[...] = p[p.shape[0] - tail.shape[0] :]
    key_grad[...] = mix[...] * value[...]


def mix_kernel(g, halo, turned, key, mix, value, turned_value, nat, wide, turn, out):
    rows, channels = g.shape
    tiles, tap_count = channels // LANES, halo.shape[0]
    for l in range(tiles):
        cols = pl.ds(l * LANES, LANES)
        nat[l, pl.ds(0, rows), :] = g[:, cols].astype(F32)
        nat[l, pl.ds(rows, tap_count), :] = halo[:, cols].astype(F32)

    @pl.loop(0, tiles)
    def _(l):
        spread(nat, l, wide, wide.shape[0], rows // 8)
        convolve(wide, turned, out, turn, l, rows // 8, False)

    for l in range(tiles):
        cols = pl.ds(l * LANES, LANES)
        m = out[l]
        mix[:, cols] = m
        v = m * key[:, cols]
        value[:, cols] = v.astype(BF16)
        turned_value[cols, :] = v.T.astype(BF16)


def filter_kernel(place, p, halo, g, kept, given, mark, nat, nat_g, wide, wide_g, halves):
    mark[...] = jnp.zeros_like(mark)
    rows, channels = g.shape
    tiles, tap_count, span = channels // LANES, halo.shape[0], g.shape[0] // 8
    core, per_half = place[2], halo.shape[0] // 2 // BLOCK
    for l in range(tiles):
        cols = pl.ds(l * LANES, LANES)
        nat[l, pl.ds(0, tap_count), :] = halo[:, cols].astype(F32)
        nat[l, pl.ds(tap_count, rows), :] = p[:, cols].astype(F32)
        nat_g[l] = g[:, cols].astype(F32)

    for l in range(tiles):
        spread(nat, l, wide, wide.shape[0], span)
        spread(nat_g, l, wide_g, span, span)

        @pl.loop(0, tap_count // BLOCK)
        def _(jb):
            zero = jnp.zeros((8, LANES), F32)
            acc = [zero] * BLOCK
            for rb in range(span // BLOCK):
                start = (rb - jb) * BLOCK + tap_count - BLOCK + 1
                window = [wide[start + i] for i in range(2 * BLOCK - 1)]
                for r in range(BLOCK):
                    up = wide_g[rb * BLOCK + r]
                    for j in range(BLOCK):
                        acc[j] = acc[j] + up * window[r - j + BLOCK - 1]
            rows_of = [jnp.sum(a, axis=0, keepdims=True) for a in acc]
            at = pl.ds(pl.multiple_of(lax.rem(jb, per_half) * BLOCK, BLOCK), BLOCK)
            half = lax.div(jb, per_half) ^ core
            halves[half, at, pl.ds(l * LANES, LANES)] = jnp.concatenate(rows_of, axis=0)

    kept[...] = halves[0]
    given[...] = halves[1]


def middle_kernel(kept, received, total, sent, mark):
    mark[...] = jnp.zeros_like(mark)
    total[...] = kept[...] + received[...].astype(F32)
    sent[...] = total[...].astype(BF16)


def conv_kernel(p, halo, upstream, turned, query_grad, mark, nat, wide, turn, out):
    mark[...] = jnp.zeros_like(mark)
    rows, channels = p.shape
    tiles, tap_count = channels // LANES, halo.shape[0]
    for l in range(tiles):
        cols = pl.ds(l * LANES, LANES)
        nat[l, pl.ds(0, tap_count), :] = halo[:, cols].astype(F32)
        nat[l, pl.ds(tap_count, rows), :] = p[:, cols].astype(F32)

    @pl.loop(0, tiles)
    def _(l):
        spread(nat, l, wide, wide.shape[0], rows // 8)
        convolve(wide, turned, out, turn, l, rows // 8, True)

    for l in range(tiles):
        cols = pl.ds(l * LANES, LANES)
        query_grad[:, cols] = upstream[:, cols].astype(F32) * out[l]


def back_kernel(place, value, held_x, weight, keep, give, values, mark, held, sems):
    mark[...] = jnp.zeros_like(mark)
    x, y, zh = place[0], place[3], place[4]
    depth = held.shape[1]
    copies = []
    order = [(out, q, h) for out in (give, keep) for q in range(2) for h in range(2)]
    owners = [y ^ (1 if out is give else 0) ^ (3 if q else 0) for out, q, h in order]
    for i, (out, q, h) in enumerate(order):
        rows = pl.ds(pl.multiple_of((owners[i] * 2 + (zh ^ h)) * depth, depth), depth)
        copies.append(pltpu.make_async_copy(weight.at[rows, :], held.at[i], sems.at[i]))
    for copy in copies:
        copy.start()
    g = value[...]
    for i, (out, q, h) in enumerate(order):
        copies[i].wait()
        part = lax.dot_general(g, held[i], (((1,), (1,)), ((), ())), preferred_element_type=F32)
        out[q, :, h * depth : (h + 1) * depth] = part.astype(out.dtype)
        block = held_x[lax.rem(owners[i] - x + 4, 4) * 2 + h]
        part = jnp.dot(block, held[i], preferred_element_type=F32)
        values[...] = part if i == 0 else values[...] + part


def pair_kernel(keep, received, own, sent, mark):
    mark[...] = jnp.zeros_like(mark)
    own[...] = keep[0] + received[0].astype(F32)
    sent[...] = (keep[1] + received[1].astype(F32)).astype(BF16)


def split_kernel(own, received, passing, staying, mark):
    mark[...] = jnp.zeros_like(mark)
    width = staying.shape[1]
    for h, out in ((0, staying), (1, passing)):
        cols = pl.ds(h * width, width)
        out[...] = (own[:, cols] + received[:, cols].astype(F32)).astype(out.dtype)


def fetch(place, blocks, held, sems):
    waits = []
    for k in range(4):
        slot = lax.rem(place[3] - place[0] - k + 8, 4)
        for phase in range(2):
            i = 2 * k + phase
            for m in range(4):

                @pl.when(slot == m)
                def _():
                    pltpu.make_async_copy(blocks[4 * phase + m], held.at[i], sems.at[i]).start()

            waits.append(pltpu.make_async_copy(blocks[0], held.at[i], sems.at[i]))
    return waits


def weight_kernel(place, *refs):
    blocks, (value, keep, give, held, mark, sems) = refs[:8], refs[8:]
    mark[...] = jnp.zeros_like(mark)
    core = place[2]
    waits = fetch(place, blocks, held, sems)
    g = value[...]
    for i in range(8):
        waits[i].wait()
        part = jnp.dot(g, held[i], preferred_element_type=F32)
        for j in range(2):
            a = part[:, 2 * j * LANES : (2 * j + 1) * LANES]
            b = part[:, (2 * j + 1) * LANES : (2 * j + 2) * LANES]
            cols = pl.ds(((i % 2) * 2 + j) * LANES, LANES)
            keep[i // 2, :, cols] = jnp.where(core == 0, a, b)
            give[i // 2, :, cols] = jnp.where(core == 0, b, a).astype(BF16)


def merge_kernel(keep, received, r0, r1, r2, r3, mark):
    mark[...] = jnp.zeros_like(mark)
    for k, r in enumerate((r0, r1, r2, r3)):
        r[...] = (keep[k] + received[k].astype(F32)).astype(r.dtype)


def gather_kernel(place, r0, r1, r2, r3, own, a1, a2, a3, mark, total):
    mark[...] = jnp.zeros_like(mark)
    zl, zh = place[1], place[4]
    for q in range(4):
        cols = pl.ds(q * LANES, LANES)
        s = r0[:, cols]
        for r in (r1, r2, r3):
            s = s + r[:, cols].astype(F32)
        total[((zh ^ (q // 2)) * 2 + q % 2) ^ zl] = s
    own[...] = total[0]
    for d, a in enumerate((a1, a2, a3)):
        a[...] = total[d + 1].astype(BF16)


def finish_kernel(scale, own, r1, r2, r3, out):
    s = own[...]
    for r in (r1, r2, r3):
        s = s + r[...].astype(F32)
    out[...] = s.T * scale


def last_kernel(own, received, out):
    out[...] = own[...] + received[...].astype(F32)


def input_kernel(staying, arrived, out):
    out[...] = staying[...].astype(F32) + arrived[...].astype(F32)


def ends_kernel(scale, place, own, other, out, both):
    half = own.shape[0]
    both[pl.ds(pl.multiple_of(place[2] * half, half), half), :] = own[...]
    both[pl.ds(pl.multiple_of((1 - place[2]) * half, half), half), :] = other[...]
    out[...] = both[...].T * scale


def shards(
    layer_input,
    value_weight,
    filter_taps,
    query_codes,
    query_low,
    query_high,
    key_codes,
    key_low,
    key_high,
    out_grad,
):
    rows, width = layer_input.shape
    channels, tap_count = filter_taps.shape
    tiles, span = channels // LANES, rows // 8
    place = jnp.stack([lax.axis_index(axis) for axis in SEQ + TP]).astype(jnp.int32)
    scale = 1.0 / math.sqrt(rows * lax.axis_size(SEQ))

    mark = struct((8, LANES), F32)
    wide_shape = pltpu.VMEM((tap_count + span, 8, LANES), F32)
    nat_shape = pltpu.VMEM((tiles, rows + tap_count, LANES), F32)
    turn_shape = pltpu.VMEM((span, 8, LANES), F32)
    out_scratch = pltpu.VMEM((tiles, rows, LANES), F32)
    plane = struct((rows, channels), F32)
    half_plane = struct((rows, channels), BF16)

    far = crossed(layer_input, "zh", 1)
    near_blocks = [layer_input] + [shifted(layer_input, "y", k) for k in (1, 2, 3)]
    grad_conv, head, key, turned = call(
        "prepare",
        prepare_kernel,
        (
            half_plane,
            struct((tap_count, channels), BF16),
            plane,
            struct((tiles, tap_count, LANES), F32),
        ),
        [("in", v) for v in (out_grad, query_codes, query_low.T, query_high.T)]
        + [("in", v) for v in (key_codes, key_low.T, key_high.T, filter_taps)],
        params=room(57),
    )
    later_rows = along_tokens(head, -1)
    far = after(far, *[("tie", b) for b in near_blocks[1:]], ("tie", later_rows))
    far_blocks = [far] + [shifted(far, "y", k) for k in (1, 2, 3)]
    grad_mix, grad_value, turned_value = call(
        "mix",
        mix_kernel,
        (plane, half_plane, struct((channels, rows), BF16)),
        [("in", grad_conv), ("in", later_rows), ("in", turned), ("in", key), ("tie", far)],
        [nat_shape, wide_shape, turn_shape, out_scratch],
        room(52),
    )

    eight = pltpu.SemaphoreType.DMA((8,))
    blocks = [("hbm", b) for b in near_blocks + far_blocks]
    keep, give, gathered, weight_mark = call(
        "weight",
        weight_kernel,
        (
            struct((4, channels, 4 * LANES), F32),
            struct((4, channels, 4 * LANES), BF16),
            struct((8, rows, width), BF16),
            mark,
        ),
        [("smem", place)] + blocks + [("vmem", turned_value)],
        [eight],
        room(40),
    )
    given_terms = crossed(give, "core", 1)
    back_keep, back_give, values, _ = call(
        "back",
        back_kernel,
        (
            struct((2, rows, 2 * width), F32),
            struct((2, rows, 2 * width), BF16),
            plane,
            mark,
        ),
        [("smem", place), ("vmem", grad_value), ("vmem", gathered), ("hbm", value_weight)]
        + [("mark", weight_mark)],
        [pltpu.VMEM((8, width, channels), BF16), eight],
        room(46),
    )
    product, tail, grad_key = call(
        "product",
        product_kernel,
        (half_plane, struct((tap_count, channels), BF16), plane),
        [("vmem", values), ("vmem", grad_mix), ("vmem", key)],
    )
    *terms, merge_mark = call(
        "merge",
        merge_kernel,
        (struct((channels, 4 * LANES), F32),)
        + (struct((channels, 4 * LANES), BF16),) * 3
        + (mark,),
        [("vmem", keep), ("in", given_terms)],
    )
    sent = [shifted(terms[k], "x", k) for k in (1, 2, 3)]
    earlier_rows = along_tokens(tail, 1)
    half_taps = struct((tap_count // 2, channels), F32)
    kept, given, taps_mark = call(
        "taps",
        filter_kernel,
        (half_taps, half_taps, mark),
        [("smem", place), ("vmem", product), ("in", earlier_rows), ("vmem", grad_conv)]
        + [("mark", merge_mark)],
        [
            nat_shape,
            out_scratch,
            wide_shape,
            pltpu.VMEM((span, 8, LANES), F32),
            pltpu.VMEM((2, tap_count // 2, channels), F32),
        ],
    )
    filter_sum, filter_sent, middle1_mark = call(
        "middle1",
        middle_kernel,
        (half_taps, struct((tap_count // 2, channels), BF16), mark),
        [("vmem", kept), ("in", crossed(given, "core", 1))],
    )
    back_own, back_sent, pair_mark = call(
        "pair",
        pair_kernel,
        (struct((rows, 2 * width), F32), struct((rows, 2 * width), BF16), mark),
        [("vmem", back_keep), ("in", crossed(back_give, "y", 1)), ("mark", middle1_mark)],
    )
    passing, staying, split_mark = call(
        "split",
        split_kernel,
        (struct((rows, width), BF16), struct((rows, width), F32), mark),
        [("vmem", back_own), ("in", crossed(back_sent, "y", 3))],
    )
    arrived_input = crossed(passing, "zh", 1)
    own, *ahead, gather_mark = call(
        "gather",
        gather_kernel,
        (struct((channels, LANES), F32),)
        + (struct((channels, LANES), BF16),) * 3
        + (mark,),
        [("smem", place), ("vmem", terms[0])]
        + [("in", v) for v in sent],
        [pltpu.VMEM((4, channels, LANES), F32)],
    )
    arrived = [crossed(ahead[d - 1], "zl", d) for d in (1, 2, 3)]
    grad_query, conv_mark = call(
        "conv",
        conv_kernel,
        (plane, mark),
        [("vmem", product), ("in", earlier_rows), ("in", out_grad), ("vmem", turned)]
        + [("mark", gather_mark), ("mark", split_mark)],
        [nat_shape, wide_shape, turn_shape, out_scratch],
    )
    filter_sum, filter_sent, middle2_mark = call(
        "middle2",
        middle_kernel,
        (half_taps, struct((tap_count // 2, channels), BF16), mark),
        [("vmem", filter_sum), ("in", crossed(filter_sent, "zl", 1))],
    )
    filter_sum, filter_sent, middle3_mark = call(
        "middle3",
        middle_kernel,
        (half_taps, struct((tap_count // 2, channels), BF16), mark),
        [("vmem", filter_sum), ("in", crossed(filter_sent, "zl", 2))]
        + [("mark", gather_mark)],
    )
    filter_sum, filter_sent, middle4_mark = call(
        "middle4",
        middle_kernel,
        (half_taps, struct((tap_count // 2, channels), BF16), mark),
        [("vmem", filter_sum), ("in", crossed(filter_sent, "x", 1))],
    )
    filter_sum = call(
        "last",
        last_kernel,
        half_taps,
        [("vmem", filter_sum), ("in", crossed(filter_sent, "x", 3))]
        + [("tie", v) for v in arrived]
        + [("mark", conv_mark)],
    )
    grad_input = call(
        "input",
        input_kernel,
        struct((rows, width), F32),
        [("vmem", staying), ("in", arrived_input)],
    )
    grad_weight = call(
        "finish",
        functools.partial(finish_kernel, scale),
        struct((LANES, channels), F32),
        [("vmem", own)]
        + [("in", v) for v in arrived]
        + [("mark", conv_mark)],
    )
    grad_filter = call(
        "ends",
        functools.partial(ends_kernel, scale),
        struct((channels, tap_count), F32),
        [("smem", place), ("vmem", filter_sum), ("in", crossed(filter_sum, "core", 1))],
        [pltpu.VMEM((tap_count, channels), F32)],
    )
    return (grad_input, grad_weight, grad_filter, grad_query, grad_key)


def solution(mesh):
    fine = Mesh(mesh.devices.reshape(4, 4, 2, 4, 2), SEQ + TP)
    both = P(SEQ, TP)
    return jax.shard_map(
        shards,
        mesh=fine,
        in_specs=(both, P(None, TP), P(TP, None)) + (both,) * 7,
        out_specs=(both, both, P(TP, None), both, both),
        check_vma=False,
    )
```

```python
import functools
import math

import jax
import jax.numpy as jnp
from jax import lax
from jax.experimental import pallas as pl
from jax.experimental.pallas import tpu as pltpu
from jax.sharding import Mesh, PartitionSpec as P

SEQ = ("x", "zl", "core")
TP = ("y", "zh")
LANES = 128
BLOCK = 16
F32 = jnp.float32
BF16 = jnp.bfloat16
VMEM = pl.BlockSpec(memory_space=pltpu.VMEM)
SMEM = pl.BlockSpec(memory_space=pltpu.SMEM)
HBM = pl.BlockSpec(memory_space=pltpu.HBM)
COST = {"prepare": 1.75, "mix": 5.39, "weight": 2.8, "back": 2.59, "pair": 0.7, "split": 0.56, "product": 0.63, "merge": 1.05, "taps": 5.6, "last":0.5,"middle1": 0.35, "middle3":0.5,"middle4":0.5,"middle2": 0.35, "gather": 1.05, "conv": 5.88, "input": 0.56, "finish": 0.91, "ends": 0.91, "after": 0.35}
PARAMS = pltpu.CompilerParams(vmem_limit_bytes=40 * 1024 * 1024)
def room(used):
    return pltpu.CompilerParams(vmem_limit_bytes=int(used * 1024 * 1024))


def shifted(block, axis, k):
    n = lax.axis_size(axis)
    return lax.ppermute(block, axis, [(i, (i + k) % n) for i in range(n)])


def crossed(block, axis, d):
    return lax.ppermute(block, axis, [(i, i ^ d) for i in range(lax.axis_size(axis))])


def along_tokens(block, step):
    n = lax.axis_size(SEQ)
    return lax.ppermute(block, SEQ, [(i, i + step) for i in range(n) if 0 <= i + step < n])


def estimate(name):
    time = COST[name]
    return pl.CostEstimate(
        flops=int(time * 1e9), bytes_accessed=int(time * 3.3e6), transcendentals=0
    )


def staged(kernel, kinds):
    count = len(kinds)
    moved = [i for i, kind in enumerate(kinds) if kind == "in"]

    def body(*refs):
        inputs, rest = list(refs[:count]), list(refs[count:])
        held, sems = rest[len(rest) - len(moved) - 1 : -1], rest[-1]
        copies = [
            pltpu.make_async_copy(inputs[i], held[n], sems.at[n]) for n, i in enumerate(moved)
        ]
        for copy in copies:
            copy.start()
        for n, i in enumerate(moved):
            inputs[i] = held[n]
        for copy in copies:
            copy.wait()
        given = [r for r, kind in zip(inputs, kinds) if kind not in ("tie", "mark")]
        kernel(*given, *rest[: len(rest) - len(moved) - 1])

    return body


SPECS = {"in": HBM, "hbm": HBM, "tie": HBM, "vmem": VMEM, "mark": VMEM, "smem": SMEM}


def call(name, kernel, out, inputs, scratch=(), params=PARAMS):
    kinds = [kind for kind, _ in inputs]
    values = [value for _, value in inputs]
    moved = [v for kind, v in inputs if kind == "in"]
    scratch = list(scratch)
    if moved:
        kernel = staged(kernel, kinds)
        scratch += [pltpu.VMEM(v.shape, v.dtype) for v in moved]
        scratch += [pltpu.SemaphoreType.DMA((len(moved),))]
    else:
        inner, keep = kernel, [i for i, k in enumerate(kinds) if k not in ("tie", "mark")]
        count = len(kinds)

        def kernel(*refs):
            inner(*[refs[i] for i in keep], *refs[count:])

    return pl.pallas_call(
        kernel,
        out_shape=out,
        in_specs=[SPECS[kind] for kind in kinds],
        out_specs=jax.tree.map(lambda _: VMEM, out),
        scratch_shapes=scratch,
        compiler_params=params,
        cost_estimate=estimate(name),
        name=name,
    )(*values)


def after(block, *waits):
    kinds = [kind for kind, _ in waits]
    return pl.pallas_call(
        lambda *refs: None,
        out_shape=struct(block.shape, block.dtype),
        in_specs=[HBM] + [SPECS[kind] for kind in kinds],
        out_specs=HBM,
        input_output_aliases={0: 0},
        compiler_params=PARAMS,
        cost_estimate=estimate("after"),
        name="after",
    )(block, *[value for _, value in waits])


def struct(shape, dtype):
    return jax.ShapeDtypeStruct(shape, dtype)


def spread(natural, tile, wide, count, span):
    step = span // 8
    for a in range(count // 8):
        rows = [natural[tile, pl.ds(8 * (a + step * q), 8), :] for q in range(8)]
        wide[pl.ds(8 * a, 8)] = jnp.swapaxes(jnp.stack(rows, 0), 0, 1)


def convolve(wide, turned, natural_out, turn, tile, span, causal):
    tap_count = turned.shape[1]
    for rb in range(span // BLOCK):

        def body(jb, acc):
            start = (rb - jb) * BLOCK + tap_count - BLOCK + 1 if causal else (rb + jb) * BLOCK
            window = [wide[start + i] for i in range(2 * BLOCK - 1)]
            acc = list(acc)
            for j in range(BLOCK):
                tap = jnp.broadcast_to(turned[tile, pl.ds(jb * BLOCK + j, 1), :], (8, LANES))
                for r in range(BLOCK):
                    acc[r] = acc[r] + tap * window[r - j + BLOCK - 1 if causal else r + j]
            return tuple(acc)

        zero = jnp.zeros((8, LANES), F32)
        acc = lax.fori_loop(0, tap_count // BLOCK, body, (zero,) * BLOCK)
        for r in range(BLOCK):
            turn[rb * BLOCK + r] = acc[r]
    for a in range(span // 8):
        eight = jnp.swapaxes(turn[pl.ds(8 * a, 8)], 0, 1)
        for q in range(8):
            natural_out[tile, pl.ds(q * span + 8 * a, 8), :] = eight[q]


def columns(low, high, codes, group):
    shape = (LANES, low.shape[1])
    bottom = jnp.broadcast_to(low[group : group + 1, :], shape).T
    step = jnp.broadcast_to((high[group : group + 1, :] - low[group : group + 1, :]) / 3.0, shape).T
    return bottom + codes[:, group * LANES : (group + 1) * LANES].astype(F32) * step


def prepare_kernel(up, codes, low, high, key_codes, key_low, key_high, taps, *outs):
    grad_conv, head, key, turned = outs
    for l in range(codes.shape[1] // LANES):
        cols = pl.ds(l * LANES, LANES)
        g = (up[:, cols].astype(F32) * columns(low, high, codes, l)).astype(BF16)
        grad_conv[:, cols] = g
        head[:, cols] = g[: head.shape[0]]
        key[:, cols] = columns(key_low, key_high, key_codes, l)
        turned[l] = taps[cols, :].astype(F32).T


def product_kernel(value, mix, key, product, tail, key_grad):
    p = (key[...] * value[...]).astype(BF16)
    product[...] = p
    tail[...] = p[p.shape[0] - tail.shape[0] :]
    key_grad[...] = mix[...] * value[...]


def mix_kernel(g, halo, turned, key, mix, value, turned_value, nat, wide, turn, out):
    rows, channels = g.shape
    tiles, tap_count = channels // LANES, halo.shape[0]
    for l in range(tiles):
        cols = pl.ds(l * LANES, LANES)
        nat[l, pl.ds(0, rows), :] = g[:, cols].astype(F32)
        nat[l, pl.ds(rows, tap_count), :] = halo[:, cols].astype(F32)

    @pl.loop(0, tiles)
    def _(l):
        spread(nat, l, wide, wide.shape[0], rows // 8)
        convolve(wide, turned, out, turn, l, rows // 8, False)

    for l in range(tiles):
        cols = pl.ds(l * LANES, LANES)
        m = out[l]
        mix[:, cols] = m
        v = m * key[:, cols]
        value[:, cols] = v.astype(BF16)
        turned_value[cols, :] = v.T.astype(BF16)


def filter_kernel(place, p, halo, g, kept, given, mark, nat, nat_g, wide, wide_g, halves):
    mark[...] = jnp.zeros_like(mark)
    rows, channels = g.shape
    tiles, tap_count, span = channels // LANES, halo.shape[0], g.shape[0] // 8
    core, per_half = place[2], halo.shape[0] // 2 // BLOCK
    for l in range(tiles):
        cols = pl.ds(l * LANES, LANES)
        nat[l, pl.ds(0, tap_count), :] = halo[:, cols].astype(F32)
        nat[l, pl.ds(tap_count, rows), :] = p[:, cols].astype(F32)
        nat_g[l] = g[:, cols].astype(F32)

    for l in range(tiles):
        spread(nat, l, wide, wide.shape[0], span)
        spread(nat_g, l, wide_g, span, span)

        @pl.loop(0, tap_count // BLOCK)
        def _(jb):
            zero = jnp.zeros((8, LANES), F32)
            acc = [zero] * BLOCK
            for rb in range(span // BLOCK):
                start = (rb - jb) * BLOCK + tap_count - BLOCK + 1
                window = [wide[start + i] for i in range(2 * BLOCK - 1)]
                for r in range(BLOCK):
                    up = wide_g[rb * BLOCK + r]
                    for j in range(BLOCK):
                        acc[j] = acc[j] + up * window[r - j + BLOCK - 1]
            rows_of = [jnp.sum(a, axis=0, keepdims=True) for a in acc]
            at = pl.ds(pl.multiple_of(lax.rem(jb, per_half) * BLOCK, BLOCK), BLOCK)
            half = lax.div(jb, per_half) ^ core
            halves[half, at, pl.ds(l * LANES, LANES)] = jnp.concatenate(rows_of, axis=0)

    kept[...] = halves[0]
    given[...] = halves[1]


def middle_kernel(kept, received, total, sent, mark):
    mark[...] = jnp.zeros_like(mark)
    total[...] = kept[...] + received[...].astype(F32)
    sent[...] = total[...].astype(BF16)


def conv_kernel(p, halo, upstream, turned, query_grad, mark, nat, wide, turn, out):
    mark[...] = jnp.zeros_like(mark)
    rows, channels = p.shape
    tiles, tap_count = channels // LANES, halo.shape[0]
    for l in range(tiles):
        cols = pl.ds(l * LANES, LANES)
        nat[l, pl.ds(0, tap_count), :] = halo[:, cols].astype(F32)
        nat[l, pl.ds(tap_count, rows), :] = p[:, cols].astype(F32)

    @pl.loop(0, tiles)
    def _(l):
        spread(nat, l, wide, wide.shape[0], rows // 8)
        convolve(wide, turned, out, turn, l, rows // 8, True)

    for l in range(tiles):
        cols = pl.ds(l * LANES, LANES)
        query_grad[:, cols] = upstream[:, cols].astype(F32) * out[l]


def back_kernel(place, value, held_x, weight, keep, give, values, mark, held, sems):
    mark[...] = jnp.zeros_like(mark)
    x, y, zh = place[0], place[3], place[4]
    depth = held.shape[1]
    copies = []
    order = [(out, q, h) for out in (give, keep) for q in range(2) for h in range(2)]
    owners = [y ^ (1 if out is give else 0) ^ (3 if q else 0) for out, q, h in order]
    for i, (out, q, h) in enumerate(order):
        rows = pl.ds(pl.multiple_of((owners[i] * 2 + (zh ^ h)) * depth, depth), depth)
        copies.append(pltpu.make_async_copy(weight.at[rows, :], held.at[i], sems.at[i]))
    for copy in copies:
        copy.start()
    g = value[...]
    for i, (out, q, h) in enumerate(order):
        copies[i].wait()
        part = lax.dot_general(g, held[i], (((1,), (1,)), ((), ())), preferred_element_type=F32)
        out[q, :, h * depth : (h + 1) * depth] = part.astype(out.dtype)
        block = held_x[lax.rem(owners[i] - x + 4, 4) * 2 + h]
        part = jnp.dot(block, held[i], preferred_element_type=F32)
        values[...] = part if i == 0 else values[...] + part


def pair_kernel(keep, received, own, sent, mark):
    mark[...] = jnp.zeros_like(mark)
    own[...] = keep[0] + received[0].astype(F32)
    sent[...] = (keep[1] + received[1].astype(F32)).astype(BF16)


def split_kernel(own, received, passing, staying, mark):
    mark[...] = jnp.zeros_like(mark)
    width = staying.shape[1]
    for h, out in ((0, staying), (1, passing)):
        cols = pl.ds(h * width, width)
        out[...] = (own[:, cols] + received[:, cols].astype(F32)).astype(out.dtype)


def fetch(place, blocks, held, sems):
    waits = []
    for k in range(4):
        slot = lax.rem(place[3] - place[0] - k + 8, 4)
        for phase in range(2):
            i = 2 * k + phase
            for m in range(4):

                @pl.when(slot == m)
                def _():
                    pltpu.make_async_copy(blocks[4 * phase + m], held.at[i], sems.at[i]).start()

            waits.append(pltpu.make_async_copy(blocks[0], held.at[i], sems.at[i]))
    return waits


def weight_kernel(place, *refs):
    blocks, (value, keep, give, held, mark, sems) = refs[:8], refs[8:]
    mark[...] = jnp.zeros_like(mark)
    core = place[2]
    waits = fetch(place, blocks, held, sems)
    g = value[...]
    for i in range(8):
        waits[i].wait()
        part = jnp.dot(g, held[i], preferred_element_type=F32)
        for j in range(2):
            a = part[:, 2 * j * LANES : (2 * j + 1) * LANES]
            b = part[:, (2 * j + 1) * LANES : (2 * j + 2) * LANES]
            cols = pl.ds(((i % 2) * 2 + j) * LANES, LANES)
            keep[i // 2, :, cols] = jnp.where(core == 0, a, b)
            give[i // 2, :, cols] = jnp.where(core == 0, b, a).astype(BF16)


def merge_kernel(keep, received, r0, r1, r2, r3, mark):
    mark[...] = jnp.zeros_like(mark)
    for k, r in enumerate((r0, r1, r2, r3)):
        r[...] = (keep[k] + received[k].astype(F32)).astype(r.dtype)


def gather_kernel(place, r0, r1, r2, r3, own, a1, a2, a3, mark, total):
    mark[...] = jnp.zeros_like(mark)
    zl, zh = place[1], place[4]
    for q in range(4):
        cols = pl.ds(q * LANES, LANES)
        s = r0[:, cols]
        for r in (r1, r2, r3):
            s = s + r[:, cols].astype(F32)
        total[((zh ^ (q // 2)) * 2 + q % 2) ^ zl] = s
    own[...] = total[0]
    for d, a in enumerate((a1, a2, a3)):
        a[...] = total[d + 1].astype(BF16)


def finish_kernel(scale, own, r1, r2, r3, out):
    s = own[...]
    for r in (r1, r2, r3):
        s = s + r[...].astype(F32)
    out[...] = s.T * scale


def last_kernel(own, received, out):
    out[...] = own[...] + received[...].astype(F32)


def input_kernel(staying, arrived, out):
    out[...] = staying[...].astype(F32) + arrived[...].astype(F32)


def ends_kernel(scale, place, own, other, out, both):
    half = own.shape[0]
    both[pl.ds(pl.multiple_of(place[2] * half, half), half), :] = own[...]
    both[pl.ds(pl.multiple_of((1 - place[2]) * half, half), half), :] = other[...]
    out[...] = both[...].T * scale


def shards(
    layer_input,
    value_weight,
    filter_taps,
    query_codes,
    query_low,
    query_high,
    key_codes,
    key_low,
    key_high,
    out_grad,
):
    rows, width = layer_input.shape
    channels, tap_count = filter_taps.shape
    tiles, span = channels // LANES, rows // 8
    place = jnp.stack([lax.axis_index(axis) for axis in SEQ + TP]).astype(jnp.int32)
    scale = 1.0 / math.sqrt(rows * lax.axis_size(SEQ))

    mark = struct((8, LANES), F32)
    wide_shape = pltpu.VMEM((tap_count + span, 8, LANES), F32)
    nat_shape = pltpu.VMEM((tiles, rows + tap_count, LANES), F32)
    turn_shape = pltpu.VMEM((span, 8, LANES), F32)
    out_scratch = pltpu.VMEM((tiles, rows, LANES), F32)
    plane = struct((rows, channels), F32)
    half_plane = struct((rows, channels), BF16)

    far = crossed(layer_input, "zh", 1)
    near_blocks = [layer_input] + [shifted(layer_input, "y", k) for k in (1, 2, 3)]
    grad_conv, head, key, turned = call(
        "prepare",
        prepare_kernel,
        (
            half_plane,
            struct((tap_count, channels), BF16),
            plane,
            struct((tiles, tap_count, LANES), F32),
        ),
        [("in", v) for v in (out_grad, query_codes, query_low.T, query_high.T)]
        + [("in", v) for v in (key_codes, key_low.T, key_high.T, filter_taps)],
        params=room(57),
    )
    later_rows = along_tokens(head, -1)
    far = after(far, ("tie", later_rows))
    far_blocks = [far] + [shifted(far, "y", k) for k in (1, 2, 3)]
    grad_mix, grad_value, turned_value = call(
        "mix",
        mix_kernel,
        (plane, half_plane, struct((channels, rows), BF16)),
        [("in", grad_conv), ("in", later_rows), ("in", turned), ("in", key), ("tie", far)]
        + [("tie", b) for b in near_blocks[1:]],
        [nat_shape, wide_shape, turn_shape, out_scratch],
        room(52),
    )

    eight = pltpu.SemaphoreType.DMA((8,))
    blocks = [("hbm", b) for b in near_blocks + far_blocks]
    keep, give, gathered, weight_mark = call(
        "weight",
        weight_kernel,
        (
            struct((4, channels, 4 * LANES), F32),
            struct((4, channels, 4 * LANES), BF16),
            struct((8, rows, width), BF16),
            mark,
        ),
        [("smem", place)] + blocks + [("vmem", turned_value)],
        [eight],
        room(40),
    )
    given_terms = crossed(give, "core", 1)
    back_keep, back_give, values, _ = call(
        "back",
        back_kernel,
        (
            struct((2, rows, 2 * width), F32),
            struct((2, rows, 2 * width), BF16),
            plane,
            mark,
        ),
        [("smem", place), ("vmem", grad_value), ("vmem", gathered), ("hbm", value_weight)]
        + [("mark", weight_mark)],
        [pltpu.VMEM((8, width, channels), BF16), eight],
        room(46),
    )
    product, tail, grad_key = call(
        "product",
        product_kernel,
        (half_plane, struct((tap_count, channels), BF16), plane),
        [("vmem", values), ("vmem", grad_mix), ("vmem", key)],
    )
    *terms, merge_mark = call(
        "merge",
        merge_kernel,
        (struct((channels, 4 * LANES), F32),)
        + (struct((channels, 4 * LANES), BF16),) * 3
        + (mark,),
        [("vmem", keep), ("in", given_terms)],
    )
    sent = [shifted(terms[k], "x", k) for k in (1, 2, 3)]
    earlier_rows = along_tokens(tail, 1)
    half_taps = struct((tap_count // 2, channels), F32)
    kept, given, taps_mark = call(
        "taps",
        filter_kernel,
        (half_taps, half_taps, mark),
        [("smem", place), ("vmem", product), ("in", earlier_rows), ("vmem", grad_conv)]
        + [("mark", merge_mark)],
        [
            nat_shape,
            out_scratch,
            wide_shape,
            pltpu.VMEM((span, 8, LANES), F32),
            pltpu.VMEM((2, tap_count // 2, channels), F32),
        ],
    )
    filter_sum, filter_sent, middle1_mark = call(
        "middle1",
        middle_kernel,
        (half_taps, struct((tap_count // 2, channels), BF16), mark),
        [("vmem", kept), ("in", crossed(given, "core", 1))],
    )
    back_own, back_sent, pair_mark = call(
        "pair",
        pair_kernel,
        (struct((rows, 2 * width), F32), struct((rows, 2 * width), BF16), mark),
        [("vmem", back_keep), ("in", crossed(back_give, "y", 1)), ("mark", middle1_mark)],
    )
    passing, staying, split_mark = call(
        "split",
        split_kernel,
        (struct((rows, width), BF16), struct((rows, width), F32), mark),
        [("vmem", back_own), ("in", crossed(back_sent, "y", 3))],
    )
    arrived_input = crossed(passing, "zh", 1)
    own, *ahead, gather_mark = call(
        "gather",
        gather_kernel,
        (struct((channels, LANES), F32),)
        + (struct((channels, LANES), BF16),) * 3
        + (mark,),
        [("smem", place), ("vmem", terms[0])]
        + [("in", v) for v in sent],
        [pltpu.VMEM((4, channels, LANES), F32)],
    )
    arrived = [crossed(ahead[d - 1], "zl", d) for d in (1, 2, 3)]
    grad_query, conv_mark = call(
        "conv",
        conv_kernel,
        (plane, mark),
        [("vmem", product), ("in", earlier_rows), ("in", out_grad), ("vmem", turned)]
        + [("mark", gather_mark), ("mark", split_mark)],
        [nat_shape, wide_shape, turn_shape, out_scratch],
    )
    filter_sum, filter_sent, middle2_mark = call(
        "middle2",
        middle_kernel,
        (half_taps, struct((tap_count // 2, channels), BF16), mark),
        [("vmem", filter_sum), ("in", crossed(filter_sent, "zl", 1))],
    )
    filter_sum, filter_sent, middle3_mark = call(
        "middle3",
        middle_kernel,
        (half_taps, struct((tap_count // 2, channels), BF16), mark),
        [("vmem", filter_sum), ("in", crossed(filter_sent, "zl", 2))]
        + [("mark", gather_mark)],
    )
    filter_sum, filter_sent, middle4_mark = call(
        "middle4",
        middle_kernel,
        (half_taps, struct((tap_count // 2, channels), BF16), mark),
        [("vmem", filter_sum), ("in", crossed(filter_sent, "x", 1))],
    )
    filter_sum = call(
        "last",
        last_kernel,
        half_taps,
        [("vmem", filter_sum), ("in", crossed(filter_sent, "x", 3))]
        + [("tie", v) for v in arrived]
        + [("mark", conv_mark)],
    )
    grad_input = call(
        "input",
        input_kernel,
        struct((rows, width), F32),
        [("vmem", staying), ("in", arrived_input)],
    )
    grad_weight = call(
        "finish",
        functools.partial(finish_kernel, scale),
        struct((LANES, channels), F32),
        [("vmem", own)]
        + [("in", v) for v in arrived]
        + [("mark", conv_mark)],
    )
    grad_filter = call(
        "ends",
        functools.partial(ends_kernel, scale),
        struct((channels, tap_count), F32),
        [("smem", place), ("vmem", filter_sum), ("in", crossed(filter_sum, "core", 1))],
        [pltpu.VMEM((tap_count, channels), F32)],
    )
    return (grad_input, grad_weight, grad_filter, grad_query, grad_key)


def solution(mesh):
    fine = Mesh(mesh.devices.reshape(4, 4, 2, 4, 2), SEQ + TP)
    both = P(SEQ, TP)
    return jax.shard_map(
        shards,
        mesh=fine,
        in_specs=(both, P(None, TP), P(TP, None)) + (both,) * 7,
        out_specs=(both, both, P(TP, None), both, both),
        check_vma=False,
    )
```

```python
import functools
import math

import jax
import jax.numpy as jnp
from jax import lax
from jax.experimental import pallas as pl
from jax.experimental.pallas import tpu as pltpu
from jax.sharding import Mesh, PartitionSpec as P

SEQ = ("x", "zl", "core")
TP = ("y", "zh")
LANES = 128
BLOCK = 16
F32 = jnp.float32
BF16 = jnp.bfloat16
VMEM = pl.BlockSpec(memory_space=pltpu.VMEM)
SMEM = pl.BlockSpec(memory_space=pltpu.SMEM)
HBM = pl.BlockSpec(memory_space=pltpu.HBM)
COST = {"prepare": 1.75, "mix": 5.39, "weight": 2.8, "back": 2.59, "pair": 0.7, "split": 0.56, "product": 0.63, "merge": 1.05, "taps": 5.6, "last":0.5,"middle1": 0.35, "middle3":0.5,"middle4":0.5,"middle2": 0.35, "gather": 1.05, "conv": 5.88, "input": 0.56, "finish": 0.91, "ends": 0.91, "after": 0.35}
PARAMS = pltpu.CompilerParams(vmem_limit_bytes=40 * 1024 * 1024)
def room(used):
    return pltpu.CompilerParams(vmem_limit_bytes=int(used * 1024 * 1024))


def shifted(block, axis, k):
    n = lax.axis_size(axis)
    return lax.ppermute(block, axis, [(i, (i + k) % n) for i in range(n)])


def crossed(block, axis, d):
    return lax.ppermute(block, axis, [(i, i ^ d) for i in range(lax.axis_size(axis))])


def along_tokens(block, step):
    n = lax.axis_size(SEQ)
    return lax.ppermute(block, SEQ, [(i, i + step) for i in range(n) if 0 <= i + step < n])


def estimate(name):
    time = COST[name]
    return pl.CostEstimate(
        flops=int(time * 1e9), bytes_accessed=int(time * 3.3e6), transcendentals=0
    )


def staged(kernel, kinds):
    count = len(kinds)
    moved = [i for i, kind in enumerate(kinds) if kind == "in"]

    def body(*refs):
        inputs, rest = list(refs[:count]), list(refs[count:])
        held, sems = rest[len(rest) - len(moved) - 1 : -1], rest[-1]
        copies = [
            pltpu.make_async_copy(inputs[i], held[n], sems.at[n]) for n, i in enumerate(moved)
        ]
        for copy in copies:
            copy.start()
        for n, i in enumerate(moved):
            inputs[i] = held[n]
        for copy in copies:
            copy.wait()
        given = [r for r, kind in zip(inputs, kinds) if kind not in ("tie", "mark")]
        kernel(*given, *rest[: len(rest) - len(moved) - 1])

    return body


SPECS = {"in": HBM, "hbm": HBM, "tie": HBM, "vmem": VMEM, "mark": VMEM, "smem": SMEM}


def call(name, kernel, out, inputs, scratch=(), params=PARAMS):
    kinds = [kind for kind, _ in inputs]
    values = [value for _, value in inputs]
    moved = [v for kind, v in inputs if kind == "in"]
    scratch = list(scratch)
    if moved:
        kernel = staged(kernel, kinds)
        scratch += [pltpu.VMEM(v.shape, v.dtype) for v in moved]
        scratch += [pltpu.SemaphoreType.DMA((len(moved),))]
    else:
        inner, keep = kernel, [i for i, k in enumerate(kinds) if k not in ("tie", "mark")]
        count = len(kinds)

        def kernel(*refs):
            inner(*[refs[i] for i in keep], *refs[count:])

    return pl.pallas_call(
        kernel,
        out_shape=out,
        in_specs=[SPECS[kind] for kind in kinds],
        out_specs=jax.tree.map(lambda _: VMEM, out),
        scratch_shapes=scratch,
        compiler_params=params,
        cost_estimate=estimate(name),
        name=name,
    )(*values)


def after(block, *waits):
    kinds = [kind for kind, _ in waits]
    return pl.pallas_call(
        lambda *refs: None,
        out_shape=struct(block.shape, block.dtype),
        in_specs=[HBM] + [SPECS[kind] for kind in kinds],
        out_specs=HBM,
        input_output_aliases={0: 0},
        compiler_params=PARAMS,
        cost_estimate=estimate("after"),
        name="after",
    )(block, *[value for _, value in waits])


def struct(shape, dtype):
    return jax.ShapeDtypeStruct(shape, dtype)


def spread(natural, tile, wide, count, span):
    step = span // 8
    for a in range(count // 8):
        rows = [natural[tile, pl.ds(8 * (a + step * q), 8), :] for q in range(8)]
        wide[pl.ds(8 * a, 8)] = jnp.swapaxes(jnp.stack(rows, 0), 0, 1)


def convolve(wide, turned, natural_out, turn, tile, span, causal):
    tap_count = turned.shape[1]
    for rb in range(span // BLOCK):

        def body(jb, acc):
            start = (rb - jb) * BLOCK + tap_count - BLOCK + 1 if causal else (rb + jb) * BLOCK
            window = [wide[start + i] for i in range(2 * BLOCK - 1)]
            acc = list(acc)
            for j in range(BLOCK):
                tap = jnp.broadcast_to(turned[tile, pl.ds(jb * BLOCK + j, 1), :], (8, LANES))
                for r in range(BLOCK):
                    acc[r] = acc[r] + tap * window[r - j + BLOCK - 1 if causal else r + j]
            return tuple(acc)

        zero = jnp.zeros((8, LANES), F32)
        acc = lax.fori_loop(0, tap_count // BLOCK, body, (zero,) * BLOCK)
        for r in range(BLOCK):
            turn[rb * BLOCK + r] = acc[r]
    for a in range(span // 8):
        eight = jnp.swapaxes(turn[pl.ds(8 * a, 8)], 0, 1)
        for q in range(8):
            natural_out[tile, pl.ds(q * span + 8 * a, 8), :] = eight[q]


def columns(low, high, codes, group):
    shape = (LANES, low.shape[1])
    bottom = jnp.broadcast_to(low[group : group + 1, :], shape).T
    step = jnp.broadcast_to((high[group : group + 1, :] - low[group : group + 1, :]) / 3.0, shape).T
    return bottom + codes[:, group * LANES : (group + 1) * LANES].astype(F32) * step


def prepare_kernel(up, codes, low, high, key_codes, key_low, key_high, taps, *outs):
    grad_conv, head, key, turned = outs
    for l in range(codes.shape[1] // LANES):
        cols = pl.ds(l * LANES, LANES)
        g = (up[:, cols].astype(F32) * columns(low, high, codes, l)).astype(BF16)
        grad_conv[:, cols] = g
        head[:, cols] = g[: head.shape[0]]
        key[:, cols] = columns(key_low, key_high, key_codes, l)
        turned[l] = taps[cols, :].astype(F32).T


def product_kernel(value, mix, key, product, tail, key_grad):
    p = (key[...] * value[...]).astype(BF16)
    product[...] = p
    tail[...] = p[p.shape[0] - tail.shape[0] :]
    key_grad[...] = mix[...] * value[...]


def mix_kernel(g, halo, turned, key, mix, value, turned_value, nat, wide, turn, out):
    rows, channels = g.shape
    tiles, tap_count = channels // LANES, halo.shape[0]
    for l in range(tiles):
        cols = pl.ds(l * LANES, LANES)
        nat[l, pl.ds(0, rows), :] = g[:, cols].astype(F32)
        nat[l, pl.ds(rows, tap_count), :] = halo[:, cols].astype(F32)

    @pl.loop(0, tiles)
    def _(l):
        spread(nat, l, wide, wide.shape[0], rows // 8)
        convolve(wide, turned, out, turn, l, rows // 8, False)

    for l in range(tiles):
        cols = pl.ds(l * LANES, LANES)
        m = out[l]
        mix[:, cols] = m
        v = m * key[:, cols]
        value[:, cols] = v.astype(BF16)
        turned_value[cols, :] = v.T.astype(BF16)


def filter_kernel(place, p, halo, g, kept, given, mark, nat, nat_g, wide, wide_g, halves):
    mark[...] = jnp.zeros_like(mark)
    rows, channels = g.shape
    tiles, tap_count, span = channels // LANES, halo.shape[0], g.shape[0] // 8
    core, per_half = place[2], halo.shape[0] // 2 // BLOCK
    for l in range(tiles):
        cols = pl.ds(l * LANES, LANES)
        nat[l, pl.ds(0, tap_count), :] = halo[:, cols].astype(F32)
        nat[l, pl.ds(tap_count, rows), :] = p[:, cols].astype(F32)
        nat_g[l] = g[:, cols].astype(F32)

    for l in range(tiles):
        spread(nat, l, wide, wide.shape[0], span)
        spread(nat_g, l, wide_g, span, span)

        @pl.loop(0, tap_count // BLOCK)
        def _(jb):
            zero = jnp.zeros((8, LANES), F32)
            acc = [zero] * BLOCK
            for rb in range(span // BLOCK):
                start = (rb - jb) * BLOCK + tap_count - BLOCK + 1
                window = [wide[start + i] for i in range(2 * BLOCK - 1)]
                for r in range(BLOCK):
                    up = wide_g[rb * BLOCK + r]
                    for j in range(BLOCK):
                        acc[j] = acc[j] + up * window[r - j + BLOCK - 1]
            rows_of = [jnp.sum(a, axis=0, keepdims=True) for a in acc]
            at = pl.ds(pl.multiple_of(lax.rem(jb, per_half) * BLOCK, BLOCK), BLOCK)
            half = lax.div(jb, per_half) ^ core
            halves[half, at, pl.ds(l * LANES, LANES)] = jnp.concatenate(rows_of, axis=0)

    kept[...] = halves[0]
    given[...] = halves[1]


def middle_kernel(kept, received, total, sent, mark):
    mark[...] = jnp.zeros_like(mark)
    total[...] = kept[...] + received[...].astype(F32)
    sent[...] = total[...].astype(BF16)


def conv_kernel(p, halo, upstream, turned, query_grad, mark, nat, wide, turn, out):
    mark[...] = jnp.zeros_like(mark)
    rows, channels = p.shape
    tiles, tap_count = channels // LANES, halo.shape[0]
    for l in range(tiles):
        cols = pl.ds(l * LANES, LANES)
        nat[l, pl.ds(0, tap_count), :] = halo[:, cols].astype(F32)
        nat[l, pl.ds(tap_count, rows), :] = p[:, cols].astype(F32)

    @pl.loop(0, tiles)
    def _(l):
        spread(nat, l, wide, wide.shape[0], rows // 8)
        convolve(wide, turned, out, turn, l, rows // 8, True)

    for l in range(tiles):
        cols = pl.ds(l * LANES, LANES)
        query_grad[:, cols] = upstream[:, cols].astype(F32) * out[l]


def back_kernel(place, value, held_x, weight, *refs):
    gives, keeps, (values, mark, held, sems) = refs[:2], refs[2:4], refs[4:]
    mark[...] = jnp.zeros_like(mark)
    x, y, zh = place[0], place[3], place[4]
    depth = held.shape[1]
    copies, owners = [], []
    order = [(give, h, q) for give in (True, False) for h in (1, 0) for q in range(2)]
    for i, (give, h, q) in enumerate(order):
        first, second = 1, 3
        owners.append(y ^ (first if give else 0) ^ (second if q else 0))
        rows = pl.ds(pl.multiple_of((owners[i] * 2 + (zh ^ h)) * depth, depth), depth)
        copies.append(pltpu.make_async_copy(weight.at[rows, :], held.at[i], sems.at[i]))
    for copy in copies:
        copy.start()
    g = value[...]
    for i, (give, h, q) in enumerate(order):
        copies[i].wait()
        part = lax.dot_general(g, held[i], (((1,), (1,)), ((), ())), preferred_element_type=F32)
        target = (gives if give else keeps)[h]
        target[q] = part.astype(target.dtype)
        block = held_x[lax.rem(owners[i] - x + 4, 4) * 2 + h]
        part = jnp.dot(block, held[i], preferred_element_type=F32)
        values[...] = part if i == 0 else values[...] + part


def pair_kernel(keep, received, *refs):
    own, sent, mark = refs[-3:] if len(refs) == 3 else refs[1:4]
    mark[...] = jnp.zeros_like(mark)
    own[...] = keep[0] + received[0].astype(F32)
    sent[...] = (keep[1] + received[1].astype(F32)).astype(BF16)
    if len(refs) > 3:
        refs[4][...] = refs[0][...]


def split_kernel(own, received, passing, mark):
    mark[...] = jnp.zeros_like(mark)
    passing[...] = (own[...] + received[...].astype(F32)).astype(BF16)


def fetch(place, blocks, held, sems):
    waits = []
    for k in range(4):
        slot = lax.rem(place[3] - place[0] - k + 8, 4)
        for phase in range(2):
            i = 2 * k + phase
            for m in range(4):

                @pl.when(slot == m)
                def _():
                    pltpu.make_async_copy(blocks[4 * phase + m], held.at[i], sems.at[i]).start()

            waits.append(pltpu.make_async_copy(blocks[0], held.at[i], sems.at[i]))
    return waits


def weight_kernel(place, *refs):
    blocks, (value, keep, give, held, mark, sems) = refs[:8], refs[8:]
    mark[...] = jnp.zeros_like(mark)
    core = place[2]
    waits = fetch(place, blocks, held, sems)
    g = value[...]
    for i in range(8):
        waits[i].wait()
        part = jnp.dot(g, held[i], preferred_element_type=F32)
        for j in range(2):
            a = part[:, 2 * j * LANES : (2 * j + 1) * LANES]
            b = part[:, (2 * j + 1) * LANES : (2 * j + 2) * LANES]
            cols = pl.ds(((i % 2) * 2 + j) * LANES, LANES)
            keep[i // 2, :, cols] = jnp.where(core == 0, a, b)
            give[i // 2, :, cols] = jnp.where(core == 0, b, a).astype(BF16)


def merge_kernel(keep, received, r0, r1, r2, r3, mark):
    mark[...] = jnp.zeros_like(mark)
    for k, r in enumerate((r0, r1, r2, r3)):
        r[...] = (keep[k] + received[k].astype(F32)).astype(r.dtype)


def gather_kernel(place, r0, r1, r2, r3, own, a1, a2, a3, mark, total):
    mark[...] = jnp.zeros_like(mark)
    zl, zh = place[1], place[4]
    for q in range(4):
        cols = pl.ds(q * LANES, LANES)
        s = r0[:, cols]
        for r in (r1, r2, r3):
            s = s + r[:, cols].astype(F32)
        total[((zh ^ (q // 2)) * 2 + q % 2) ^ zl] = s
    own[...] = total[0]
    for d, a in enumerate((a1, a2, a3)):
        a[...] = total[d + 1].astype(BF16)


def finish_kernel(scale, own, r1, r2, r3, out):
    s = own[...]
    for r in (r1, r2, r3):
        s = s + r[...].astype(F32)
    out[...] = s.T * scale


def last_kernel(own, received, out):
    out[...] = own[...] + received[...].astype(F32)


def input_kernel(own, received, arrived, out):
    out[...] = own[...] + received[...].astype(F32) + arrived[...].astype(F32)


def ends_kernel(scale, place, own, other, out, both):
    half = own.shape[0]
    both[pl.ds(pl.multiple_of(place[2] * half, half), half), :] = own[...]
    both[pl.ds(pl.multiple_of((1 - place[2]) * half, half), half), :] = other[...]
    out[...] = both[...].T * scale


def shards(
    layer_input,
    value_weight,
    filter_taps,
    query_codes,
    query_low,
    query_high,
    key_codes,
    key_low,
    key_high,
    out_grad,
):
    rows, width = layer_input.shape
    channels, tap_count = filter_taps.shape
    tiles, span = channels // LANES, rows // 8
    place = jnp.stack([lax.axis_index(axis) for axis in SEQ + TP]).astype(jnp.int32)
    scale = 1.0 / math.sqrt(rows * lax.axis_size(SEQ))

    mark = struct((8, LANES), F32)
    wide_shape = pltpu.VMEM((tap_count + span, 8, LANES), F32)
    nat_shape = pltpu.VMEM((tiles, rows + tap_count, LANES), F32)
    turn_shape = pltpu.VMEM((span, 8, LANES), F32)
    out_scratch = pltpu.VMEM((tiles, rows, LANES), F32)
    plane = struct((rows, channels), F32)
    half_plane = struct((rows, channels), BF16)

    far = crossed(layer_input, "zh", 1)
    near_blocks = [layer_input] + [shifted(layer_input, "y", k) for k in (1, 2, 3)]
    grad_conv, head, key, turned = call(
        "prepare",
        prepare_kernel,
        (
            half_plane,
            struct((tap_count, channels), BF16),
            plane,
            struct((tiles, tap_count, LANES), F32),
        ),
        [("in", v) for v in (out_grad, query_codes, query_low.T, query_high.T)]
        + [("in", v) for v in (key_codes, key_low.T, key_high.T, filter_taps)],
        params=room(57),
    )
    later_rows = along_tokens(head, -1)
    far = after(far, ("tie", later_rows))
    far_blocks = [far] + [shifted(far, "y", k) for k in (1, 2, 3)]
    grad_mix, grad_value, turned_value = call(
        "mix",
        mix_kernel,
        (plane, half_plane, struct((channels, rows), BF16)),
        [("in", grad_conv), ("in", later_rows), ("in", turned), ("in", key), ("tie", far)]
        + [("tie", b) for b in near_blocks[1:]],
        [nat_shape, wide_shape, turn_shape, out_scratch],
        room(52),
    )

    eight = pltpu.SemaphoreType.DMA((8,))
    blocks = [("hbm", b) for b in near_blocks + far_blocks]
    keep, give, gathered, weight_mark = call(
        "weight",
        weight_kernel,
        (
            struct((4, channels, 4 * LANES), F32),
            struct((4, channels, 4 * LANES), BF16),
            struct((8, rows, width), BF16),
            mark,
        ),
        [("smem", place)] + blocks + [("vmem", turned_value)],
        [eight],
        room(40),
    )
    given_terms = crossed(give, "core", 1)
    give0, give1, keep0, keep1, values, _ = call(
        "back",
        back_kernel,
        (struct((2, rows, width), BF16),) * 2
        + (struct((2, rows, width), F32),) * 2
        + (plane, mark),
        [("smem", place), ("vmem", grad_value), ("vmem", gathered), ("hbm", value_weight)]
        + [("mark", weight_mark)],
        [pltpu.VMEM((8, width, channels), BF16), eight],
        room(46),
    )
    product, tail, grad_key = call(
        "product",
        product_kernel,
        (half_plane, struct((tap_count, channels), BF16), plane),
        [("vmem", values), ("vmem", grad_mix), ("vmem", key)],
    )
    *terms, merge_mark = call(
        "merge",
        merge_kernel,
        (struct((channels, 4 * LANES), F32),)
        + (struct((channels, 4 * LANES), BF16),) * 3
        + (mark,),
        [("vmem", keep), ("in", given_terms)],
    )
    sent = [shifted(terms[k], "x", k) for k in (1, 2, 3)]
    earlier_rows = along_tokens(tail, 1)
    half_taps = struct((tap_count // 2, channels), F32)
    kept, given, taps_mark = call(
        "taps",
        filter_kernel,
        (half_taps, half_taps, mark),
        [("smem", place), ("vmem", product), ("in", earlier_rows), ("vmem", grad_conv)]
        + [("mark", merge_mark)],
        [
            nat_shape,
            out_scratch,
            wide_shape,
            pltpu.VMEM((span, 8, LANES), F32),
            pltpu.VMEM((2, tap_count // 2, channels), F32),
        ],
    )
    filter_sum, filter_sent, middle1_mark = call(
        "middle1",
        middle_kernel,
        (half_taps, struct((tap_count // 2, channels), BF16), mark),
        [("vmem", kept), ("in", crossed(given, "core", 1))],
    )
    block, half_block = struct((rows, width), F32), struct((rows, width), BF16)
    own1, sent1, _, give0 = call(
        "pair",
        pair_kernel,
        (block, half_block, mark, struct((2, rows, width), BF16)),
        [("vmem", keep1), ("in", crossed(give1, "y", 1)), ("vmem", give0)]
        + [("mark", taps_mark)],
    )
    received0 = crossed(give0, "y", 1)
    passing, split_mark = call(
        "split",
        split_kernel,
        (half_block, mark),
        [("vmem", own1), ("in", crossed(sent1, "y", 3))],
    )
    arrived_input = crossed(passing, "zh", 1)
    own, *ahead, gather_mark = call(
        "gather",
        gather_kernel,
        (struct((channels, LANES), F32),)
        + (struct((channels, LANES), BF16),) * 3
        + (mark,),
        [("smem", place), ("vmem", terms[0])]
        + [("in", v) for v in sent]
        + [("mark", split_mark)],
        [pltpu.VMEM((4, channels, LANES), F32)],
    )
    arrived = [crossed(ahead[d - 1], "zl", d) for d in (1, 2, 3)]
    grad_query, conv_mark = call(
        "conv",
        conv_kernel,
        (plane, mark),
        [("vmem", product), ("in", earlier_rows), ("in", out_grad), ("vmem", turned)]
        + [("mark", gather_mark)],
        [nat_shape, wide_shape, turn_shape, out_scratch],
    )
    filter_sum, filter_sent, middle2_mark = call(
        "middle2",
        middle_kernel,
        (half_taps, struct((tap_count // 2, channels), BF16), mark),
        [("vmem", filter_sum), ("in", crossed(filter_sent, "zl", 1))],
    )
    filter_sum, filter_sent, middle3_mark = call(
        "middle3",
        middle_kernel,
        (half_taps, struct((tap_count // 2, channels), BF16), mark),
        [("vmem", filter_sum), ("in", crossed(filter_sent, "zl", 2))]
        + [("mark", gather_mark)],
    )
    filter_sum, filter_sent, middle4_mark = call(
        "middle4",
        middle_kernel,
        (half_taps, struct((tap_count // 2, channels), BF16), mark),
        [("vmem", filter_sum), ("in", crossed(filter_sent, "x", 1))]
        + [("tie", arrived_input)],
    )
    filter_sum = call(
        "last",
        last_kernel,
        half_taps,
        [("vmem", filter_sum), ("in", crossed(filter_sent, "x", 3))]
        + [("tie", v) for v in arrived]
        + [("mark", conv_mark)],
    )
    own0, sent0, pair_mark = call(
        "pair",
        pair_kernel,
        (block, half_block, mark),
        [("vmem", keep0), ("in", received0), ("mark", gather_mark)],
    )
    grad_input = call(
        "input",
        input_kernel,
        block,
        [("vmem", own0), ("in", crossed(sent0, "y", 3)), ("in", arrived_input)],
    )
    grad_weight = call(
        "finish",
        functools.partial(finish_kernel, scale),
        struct((LANES, channels), F32),
        [("vmem", own)]
        + [("in", v) for v in arrived]
        + [("mark", conv_mark)],
    )
    grad_filter = call(
        "ends",
        functools.partial(ends_kernel, scale),
        struct((channels, tap_count), F32),
        [("smem", place), ("vmem", filter_sum), ("in", crossed(filter_sum, "core", 1))],
        [pltpu.VMEM((tap_count, channels), F32)],
    )
    return (grad_input, grad_weight, grad_filter, grad_query, grad_key)


def solution(mesh):
    fine = Mesh(mesh.devices.reshape(4, 4, 2, 4, 2), SEQ + TP)
    both = P(SEQ, TP)
    return jax.shard_map(
        shards,
        mesh=fine,
        in_specs=(both, P(None, TP), P(TP, None)) + (both,) * 7,
        out_specs=(both, both, P(TP, None), both, both),
        check_vma=False,
    )
```

```python
import functools
import math

import jax
import jax.numpy as jnp
from jax import lax
from jax.experimental import pallas as pl
from jax.experimental.pallas import tpu as pltpu
from jax.sharding import Mesh, PartitionSpec as P

SEQ = ("x", "zl", "core")
TP = ("y", "zh")
LANES = 128
BLOCK = 16
F32 = jnp.float32
BF16 = jnp.bfloat16
VMEM = pl.BlockSpec(memory_space=pltpu.VMEM)
SMEM = pl.BlockSpec(memory_space=pltpu.SMEM)
HBM = pl.BlockSpec(memory_space=pltpu.HBM)
COST = {"prepare": 1.75, "mix": 5.39, "weight": 2.8, "back": 2.59, "pair": 0.7, "split": 0.56, "product": 0.63, "merge": 1.05, "taps": 5.6, "last":0.5,"middle1": 0.35, "middle3":0.5,"middle4":0.5,"middle2": 0.35, "gather": 1.05, "conv": 5.88, "input": 0.56, "finish": 0.91, "ends": 0.91, "after": 0.35}
PARAMS = pltpu.CompilerParams(vmem_limit_bytes=40 * 1024 * 1024)
def room(used):
    return pltpu.CompilerParams(vmem_limit_bytes=int(used * 1024 * 1024))


def shifted(block, axis, k):
    n = lax.axis_size(axis)
    return lax.ppermute(block, axis, [(i, (i + k) % n) for i in range(n)])


def crossed(block, axis, d):
    return lax.ppermute(block, axis, [(i, i ^ d) for i in range(lax.axis_size(axis))])


def along_tokens(block, step):
    n = lax.axis_size(SEQ)
    return lax.ppermute(block, SEQ, [(i, i + step) for i in range(n) if 0 <= i + step < n])


def estimate(name):
    time = COST[name]
    return pl.CostEstimate(
        flops=int(time * 1e9), bytes_accessed=int(time * 3.3e6), transcendentals=0
    )


def staged(kernel, kinds):
    count = len(kinds)
    moved = [i for i, kind in enumerate(kinds) if kind == "in"]

    def body(*refs):
        inputs, rest = list(refs[:count]), list(refs[count:])
        held, sems = rest[len(rest) - len(moved) - 1 : -1], rest[-1]
        copies = [
            pltpu.make_async_copy(inputs[i], held[n], sems.at[n]) for n, i in enumerate(moved)
        ]
        for copy in copies:
            copy.start()
        for n, i in enumerate(moved):
            inputs[i] = held[n]
        for copy in copies:
            copy.wait()
        given = [r for r, kind in zip(inputs, kinds) if kind not in ("tie", "mark")]
        kernel(*given, *rest[: len(rest) - len(moved) - 1])

    return body


SPECS = {"in": HBM, "hbm": HBM, "tie": HBM, "vmem": VMEM, "mark": VMEM, "smem": SMEM}


def call(name, kernel, out, inputs, scratch=(), params=PARAMS):
    kinds = [kind for kind, _ in inputs]
    values = [value for _, value in inputs]
    moved = [v for kind, v in inputs if kind == "in"]
    scratch = list(scratch)
    if moved:
        kernel = staged(kernel, kinds)
        scratch += [pltpu.VMEM(v.shape, v.dtype) for v in moved]
        scratch += [pltpu.SemaphoreType.DMA((len(moved),))]
    else:
        inner, keep = kernel, [i for i, k in enumerate(kinds) if k not in ("tie", "mark")]
        count = len(kinds)

        def kernel(*refs):
            inner(*[refs[i] for i in keep], *refs[count:])

    return pl.pallas_call(
        kernel,
        out_shape=out,
        in_specs=[SPECS[kind] for kind in kinds],
        out_specs=jax.tree.map(lambda _: VMEM, out),
        scratch_shapes=scratch,
        compiler_params=params,
        cost_estimate=estimate(name),
        name=name,
    )(*values)


def after(block, *waits):
    kinds = [kind for kind, _ in waits]
    return pl.pallas_call(
        lambda *refs: None,
        out_shape=struct(block.shape, block.dtype),
        in_specs=[HBM] + [SPECS[kind] for kind in kinds],
        out_specs=HBM,
        input_output_aliases={0: 0},
        compiler_params=PARAMS,
        cost_estimate=estimate("after"),
        name="after",
    )(block, *[value for _, value in waits])


def struct(shape, dtype):
    return jax.ShapeDtypeStruct(shape, dtype)


def spread(natural, tile, wide, count, span):
    step = span // 8
    for a in range(count // 8):
        rows = [natural[tile, pl.ds(8 * (a + step * q), 8), :] for q in range(8)]
        wide[pl.ds(8 * a, 8)] = jnp.swapaxes(jnp.stack(rows, 0), 0, 1)


def convolve(wide, turned, natural_out, turn, tile, span, causal):
    tap_count = turned.shape[1]
    for rb in range(span // BLOCK):

        def body(jb, acc):
            start = (rb - jb) * BLOCK + tap_count - BLOCK + 1 if causal else (rb + jb) * BLOCK
            window = [wide[start + i] for i in range(2 * BLOCK - 1)]
            acc = list(acc)
            for j in range(BLOCK):
                tap = jnp.broadcast_to(turned[tile, pl.ds(jb * BLOCK + j, 1), :], (8, LANES))
                for r in range(BLOCK):
                    acc[r] = acc[r] + tap * window[r - j + BLOCK - 1 if causal else r + j]
            return tuple(acc)

        zero = jnp.zeros((8, LANES), F32)
        acc = lax.fori_loop(0, tap_count // BLOCK, body, (zero,) * BLOCK)
        for r in range(BLOCK):
            turn[rb * BLOCK + r] = acc[r]
    for a in range(span // 8):
        eight = jnp.swapaxes(turn[pl.ds(8 * a, 8)], 0, 1)
        for q in range(8):
            natural_out[tile, pl.ds(q * span + 8 * a, 8), :] = eight[q]


def columns(low, high, codes, group):
    shape = (LANES, low.shape[1])
    bottom = jnp.broadcast_to(low[group : group + 1, :], shape).T
    step = jnp.broadcast_to((high[group : group + 1, :] - low[group : group + 1, :]) / 3.0, shape).T
    return bottom + codes[:, group * LANES : (group + 1) * LANES].astype(F32) * step


def prepare_kernel(up, codes, low, high, key_codes, key_low, key_high, taps, *outs):
    grad_conv, head, key, turned = outs
    for l in range(codes.shape[1] // LANES):
        cols = pl.ds(l * LANES, LANES)
        g = (up[:, cols].astype(F32) * columns(low, high, codes, l)).astype(BF16)
        grad_conv[:, cols] = g
        head[:, cols] = g[: head.shape[0]]
        key[:, cols] = columns(key_low, key_high, key_codes, l)
        turned[l] = taps[cols, :].astype(F32).T


def product_kernel(value, mix, key, product, tail, key_grad):
    p = (key[...] * value[...]).astype(BF16)
    product[...] = p
    tail[...] = p[p.shape[0] - tail.shape[0] :]
    key_grad[...] = mix[...] * value[...]


def mix_kernel(g, halo, turned, key, mix, value, turned_value, nat, wide, turn, out):
    rows, channels = g.shape
    tiles, tap_count = channels // LANES, halo.shape[0]
    for l in range(tiles):
        cols = pl.ds(l * LANES, LANES)
        nat[l, pl.ds(0, rows), :] = g[:, cols].astype(F32)
        nat[l, pl.ds(rows, tap_count), :] = halo[:, cols].astype(F32)

    @pl.loop(0, tiles)
    def _(l):
        spread(nat, l, wide, wide.shape[0], rows // 8)
        convolve(wide, turned, out, turn, l, rows // 8, False)

    for l in range(tiles):
        cols = pl.ds(l * LANES, LANES)
        m = out[l]
        mix[:, cols] = m
        v = m * key[:, cols]
        value[:, cols] = v.astype(BF16)
        turned_value[cols, :] = v.T.astype(BF16)


def filter_kernel(place, p, halo, g, kept, given, mark, nat, nat_g, wide, wide_g, halves):
    mark[...] = jnp.zeros_like(mark)
    rows, channels = g.shape
    tiles, tap_count, span = channels // LANES, halo.shape[0], g.shape[0] // 8
    core, per_half = place[2], halo.shape[0] // 2 // BLOCK
    for l in range(tiles):
        cols = pl.ds(l * LANES, LANES)
        nat[l, pl.ds(0, tap_count), :] = halo[:, cols].astype(F32)
        nat[l, pl.ds(tap_count, rows), :] = p[:, cols].astype(F32)
        nat_g[l] = g[:, cols].astype(F32)

    for l in range(tiles):
        spread(nat, l, wide, wide.shape[0], span)
        spread(nat_g, l, wide_g, span, span)

        @pl.loop(0, tap_count // BLOCK)
        def _(jb):
            zero = jnp.zeros((8, LANES), F32)
            acc = [zero] * BLOCK
            for rb in range(span // BLOCK):
                start = (rb - jb) * BLOCK + tap_count - BLOCK + 1
                window = [wide[start + i] for i in range(2 * BLOCK - 1)]
                for r in range(BLOCK):
                    up = wide_g[rb * BLOCK + r]
                    for j in range(BLOCK):
                        acc[j] = acc[j] + up * window[r - j + BLOCK - 1]
            rows_of = [jnp.sum(a, axis=0, keepdims=True) for a in acc]
            at = pl.ds(pl.multiple_of(lax.rem(jb, per_half) * BLOCK, BLOCK), BLOCK)
            half = lax.div(jb, per_half) ^ core
            halves[half, at, pl.ds(l * LANES, LANES)] = jnp.concatenate(rows_of, axis=0)

    kept[...] = halves[0]
    given[...] = halves[1]


def middle_kernel(kept, received, total, sent, mark):
    mark[...] = jnp.zeros_like(mark)
    total[...] = kept[...] + received[...].astype(F32)
    sent[...] = total[...].astype(BF16)


def conv_kernel(p, halo, upstream, turned, query_grad, mark, nat, wide, turn, out):
    mark[...] = jnp.zeros_like(mark)
    rows, channels = p.shape
    tiles, tap_count = channels // LANES, halo.shape[0]
    for l in range(tiles):
        cols = pl.ds(l * LANES, LANES)
        nat[l, pl.ds(0, tap_count), :] = halo[:, cols].astype(F32)
        nat[l, pl.ds(tap_count, rows), :] = p[:, cols].astype(F32)

    @pl.loop(0, tiles)
    def _(l):
        spread(nat, l, wide, wide.shape[0], rows // 8)
        convolve(wide, turned, out, turn, l, rows // 8, True)

    for l in range(tiles):
        cols = pl.ds(l * LANES, LANES)
        query_grad[:, cols] = upstream[:, cols].astype(F32) * out[l]


def back_kernel(place, value, held_x, weight, *refs):
    gives, keeps, (values, mark, held, sems) = refs[:2], refs[2:4], refs[4:]
    mark[...] = jnp.zeros_like(mark)
    x, y, zh = place[0], place[3], place[4]
    depth = held.shape[1]
    copies, owners = [], []
    order = [(give, h, q) for give in (True, False) for h in (1, 0) for q in range(2)]
    for i, (give, h, q) in enumerate(order):
        first, second = 1, 3
        owners.append(y ^ (first if give else 0) ^ (second if q else 0))
        rows = pl.ds(pl.multiple_of((owners[i] * 2 + (zh ^ h)) * depth, depth), depth)
        copies.append(pltpu.make_async_copy(weight.at[rows, :], held.at[i], sems.at[i]))
    for copy in copies:
        copy.start()
    g = value[...]
    for i, (give, h, q) in enumerate(order):
        copies[i].wait()
        part = lax.dot_general(g, held[i], (((1,), (1,)), ((), ())), preferred_element_type=F32)
        target = (gives if give else keeps)[h]
        target[q] = part.astype(target.dtype)
        block = held_x[lax.rem(owners[i] - x + 4, 4) * 2 + h]
        part = jnp.dot(block, held[i], preferred_element_type=F32)
        values[...] = part if i == 0 else values[...] + part


def pair_kernel(keep, received, *refs):
    own, sent, mark = refs[-3:] if len(refs) == 3 else refs[1:4]
    mark[...] = jnp.zeros_like(mark)
    own[...] = keep[0] + received[0].astype(F32)
    sent[...] = (keep[1] + received[1].astype(F32)).astype(BF16)
    if len(refs) > 3:
        refs[4][...] = refs[0][...]


def split_kernel(own, received, passing, mark):
    mark[...] = jnp.zeros_like(mark)
    passing[...] = (own[...] + received[...].astype(F32)).astype(BF16)


def fetch(place, blocks, held, sems):
    waits = []
    for k in range(4):
        slot = lax.rem(place[3] - place[0] - k + 8, 4)
        for phase in range(2):
            i = 2 * k + phase
            for m in range(4):

                @pl.when(slot == m)
                def _():
                    pltpu.make_async_copy(blocks[4 * phase + m], held.at[i], sems.at[i]).start()

            waits.append(pltpu.make_async_copy(blocks[0], held.at[i], sems.at[i]))
    return waits


def weight_kernel(place, *refs):
    blocks, (value, keep, give, held, mark, sems) = refs[:8], refs[8:]
    mark[...] = jnp.zeros_like(mark)
    core = place[2]
    waits = fetch(place, blocks, held, sems)
    g = value[...]
    for i in range(8):
        waits[i].wait()
        part = jnp.dot(g, held[i], preferred_element_type=F32)
        for j in range(2):
            a = part[:, 2 * j * LANES : (2 * j + 1) * LANES]
            b = part[:, (2 * j + 1) * LANES : (2 * j + 2) * LANES]
            cols = pl.ds(((i % 2) * 2 + j) * LANES, LANES)
            keep[i // 2, :, cols] = jnp.where(core == 0, a, b)
            give[i // 2, :, cols] = jnp.where(core == 0, b, a).astype(BF16)


def merge_kernel(keep, received, r0, r1, r2, r3, mark):
    mark[...] = jnp.zeros_like(mark)
    for k, r in enumerate((r0, r1, r2, r3)):
        r[...] = (keep[k] + received[k].astype(F32)).astype(r.dtype)


def gather_kernel(place, r0, r1, r2, r3, own, a1, a2, a3, mark, total):
    mark[...] = jnp.zeros_like(mark)
    zl, zh = place[1], place[4]
    for q in range(4):
        cols = pl.ds(q * LANES, LANES)
        s = r0[:, cols]
        for r in (r1, r2, r3):
            s = s + r[:, cols].astype(F32)
        total[((zh ^ (q // 2)) * 2 + q % 2) ^ zl] = s
    own[...] = total[0]
    for d, a in enumerate((a1, a2, a3)):
        a[...] = total[d + 1].astype(BF16)


def finish_kernel(scale, own, r1, r2, r3, out):
    s = own[...]
    for r in (r1, r2, r3):
        s = s + r[...].astype(F32)
    out[...] = s.T * scale


def last_kernel(own, received, out):
    out[...] = own[...] + received[...].astype(F32)


def input_kernel(own, received, arrived, out):
    out[...] = own[...] + received[...].astype(F32) + arrived[...].astype(F32)


def ends_kernel(scale, place, own, other, out, both):
    half = own.shape[0]
    both[pl.ds(pl.multiple_of(place[2] * half, half), half), :] = own[...]
    both[pl.ds(pl.multiple_of((1 - place[2]) * half, half), half), :] = other[...]
    out[...] = both[...].T * scale


def shards(
    layer_input,
    value_weight,
    filter_taps,
    query_codes,
    query_low,
    query_high,
    key_codes,
    key_low,
    key_high,
    out_grad,
):
    rows, width = layer_input.shape
    channels, tap_count = filter_taps.shape
    tiles, span = channels // LANES, rows // 8
    place = jnp.stack([lax.axis_index(axis) for axis in SEQ + TP]).astype(jnp.int32)
    scale = 1.0 / math.sqrt(rows * lax.axis_size(SEQ))

    mark = struct((8, LANES), F32)
    wide_shape = pltpu.VMEM((tap_count + span, 8, LANES), F32)
    nat_shape = pltpu.VMEM((tiles, rows + tap_count, LANES), F32)
    turn_shape = pltpu.VMEM((span, 8, LANES), F32)
    out_scratch = pltpu.VMEM((tiles, rows, LANES), F32)
    plane = struct((rows, channels), F32)
    half_plane = struct((rows, channels), BF16)

    far = crossed(layer_input, "zh", 1)
    near_blocks = [layer_input] + [shifted(layer_input, "y", k) for k in (1, 2, 3)]
    grad_conv, head, key, turned = call(
        "prepare",
        prepare_kernel,
        (
            half_plane,
            struct((tap_count, channels), BF16),
            plane,
            struct((tiles, tap_count, LANES), F32),
        ),
        [("in", v) for v in (out_grad, query_codes, query_low.T, query_high.T)]
        + [("in", v) for v in (key_codes, key_low.T, key_high.T, filter_taps)],
        params=room(57),
    )
    later_rows = along_tokens(head, -1)
    far = after(far, ("tie", later_rows))
    far_blocks = [far] + [shifted(far, "y", k) for k in (1, 2, 3)]
    grad_mix, grad_value, turned_value = call(
        "mix",
        mix_kernel,
        (plane, half_plane, struct((channels, rows), BF16)),
        [("in", grad_conv), ("in", later_rows), ("in", turned), ("in", key), ("tie", far)]
        + [("tie", b) for b in near_blocks[1:]],
        [nat_shape, wide_shape, turn_shape, out_scratch],
        room(52),
    )

    eight = pltpu.SemaphoreType.DMA((8,))
    blocks = [("hbm", b) for b in near_blocks + far_blocks]
    keep, give, gathered, weight_mark = call(
        "weight",
        weight_kernel,
        (
            struct((4, channels, 4 * LANES), F32),
            struct((4, channels, 4 * LANES), BF16),
            struct((8, rows, width), BF16),
            mark,
        ),
        [("smem", place)] + blocks + [("vmem", turned_value)],
        [eight],
        room(40),
    )
    given_terms = crossed(give, "core", 1)
    give0, give1, keep0, keep1, values, _ = call(
        "back",
        back_kernel,
        (struct((2, rows, width), BF16),) * 2
        + (struct((2, rows, width), F32),) * 2
        + (plane, mark),
        [("smem", place), ("vmem", grad_value), ("vmem", gathered), ("hbm", value_weight)]
        + [("mark", weight_mark)],
        [pltpu.VMEM((8, width, channels), BF16), eight],
        room(46),
    )
    product, tail, grad_key = call(
        "product",
        product_kernel,
        (half_plane, struct((tap_count, channels), BF16), plane),
        [("vmem", values), ("vmem", grad_mix), ("vmem", key)],
    )
    *terms, merge_mark = call(
        "merge",
        merge_kernel,
        (struct((channels, 4 * LANES), F32),)
        + (struct((channels, 4 * LANES), BF16),) * 3
        + (mark,),
        [("vmem", keep), ("in", given_terms)],
    )
    sent = [shifted(terms[k], "x", k) for k in (1, 2, 3)]
    earlier_rows = along_tokens(tail, 1)
    half_taps = struct((tap_count // 2, channels), F32)
    kept, given, taps_mark = call(
        "taps",
        filter_kernel,
        (half_taps, half_taps, mark),
        [("smem", place), ("vmem", product), ("in", earlier_rows), ("vmem", grad_conv)]
        + [("mark", merge_mark)],
        [
            nat_shape,
            out_scratch,
            wide_shape,
            pltpu.VMEM((span, 8, LANES), F32),
            pltpu.VMEM((2, tap_count // 2, channels), F32),
        ],
    )
    filter_sum, filter_sent, middle1_mark = call(
        "middle1",
        middle_kernel,
        (half_taps, struct((tap_count // 2, channels), BF16), mark),
        [("vmem", kept), ("in", crossed(given, "core", 1))],
    )
    block, half_block = struct((rows, width), F32), struct((rows, width), BF16)
    own1, sent1, _, give0 = call(
        "pair",
        pair_kernel,
        (block, half_block, mark, struct((2, rows, width), BF16)),
        [("vmem", keep1), ("in", crossed(give1, "y", 1)), ("vmem", give0)]
        + [("mark", taps_mark)],
    )
    received0 = crossed(give0, "y", 1)
    passing, split_mark = call(
        "split",
        split_kernel,
        (half_block, mark),
        [("vmem", own1), ("in", crossed(sent1, "y", 3))],
    )
    arrived_input = crossed(passing, "zh", 1)
    own, *ahead, gather_mark = call(
        "gather",
        gather_kernel,
        (struct((channels, LANES), F32),)
        + (struct((channels, LANES), BF16),) * 3
        + (mark,),
        [("smem", place), ("vmem", terms[0])]
        + [("in", v) for v in sent]
        + [("mark", split_mark)],
        [pltpu.VMEM((4, channels, LANES), F32)],
    )
    arrived = [crossed(ahead[d - 1], "zl", d) for d in (1, 2, 3)]
    grad_query, conv_mark = call(
        "conv",
        conv_kernel,
        (plane, mark),
        [("vmem", product), ("in", earlier_rows), ("in", out_grad), ("vmem", turned)]
        + [("mark", gather_mark)],
        [nat_shape, wide_shape, turn_shape, out_scratch],
    )
    filter_sum, filter_sent, middle2_mark = call(
        "middle2",
        middle_kernel,
        (half_taps, struct((tap_count // 2, channels), BF16), mark),
        [("vmem", filter_sum), ("in", crossed(filter_sent, "zl", 1))],
    )
    filter_sum, filter_sent, middle3_mark = call(
        "middle3",
        middle_kernel,
        (half_taps, struct((tap_count // 2, channels), BF16), mark),
        [("vmem", filter_sum), ("in", crossed(filter_sent, "zl", 2))]
        + [("mark", conv_mark)] + [("tie", v) for v in arrived[:1]],
    )
    filter_sum, filter_sent, middle4_mark = call(
        "middle4",
        middle_kernel,
        (half_taps, struct((tap_count // 2, channels), BF16), mark),
        [("vmem", filter_sum), ("in", crossed(filter_sent, "x", 1))]
        + [("tie", arrived_input)],
    )
    filter_sum = call(
        "last",
        last_kernel,
        half_taps,
        [("vmem", filter_sum), ("in", crossed(filter_sent, "x", 3))]
        + [("tie", v) for v in arrived]
        + [("mark", conv_mark)],
    )
    own0, sent0, pair_mark = call(
        "pair",
        pair_kernel,
        (block, half_block, mark),
        [("vmem", keep0), ("in", received0), ("mark", gather_mark)],
    )
    grad_input = call(
        "input",
        input_kernel,
        block,
        [("vmem", own0), ("in", crossed(sent0, "y", 3)), ("in", arrived_input)],
    )
    grad_weight = call(
        "finish",
        functools.partial(finish_kernel, scale),
        struct((LANES, channels), F32),
        [("vmem", own)]
        + [("in", v) for v in arrived]
        + [("mark", conv_mark)],
    )
    grad_filter = call(
        "ends",
        functools.partial(ends_kernel, scale),
        struct((channels, tap_count), F32),
        [("smem", place), ("vmem", filter_sum), ("in", crossed(filter_sum, "core", 1))],
        [pltpu.VMEM((tap_count, channels), F32)],
    )
    return (grad_input, grad_weight, grad_filter, grad_query, grad_key)


def solution(mesh):
    fine = Mesh(mesh.devices.reshape(4, 4, 2, 4, 2), SEQ + TP)
    both = P(SEQ, TP)
    return jax.shard_map(
        shards,
        mesh=fine,
        in_specs=(both, P(None, TP), P(TP, None)) + (both,) * 7,
        out_specs=(both, both, P(TP, None), both, both),
        check_vma=False,
    )
```
